512 devices in a mesh: seq: 64 (over z, y), tp: 8 (over x, core).
Axes of the slice: x: 4, y: 4, z: 16, core: 2. Of those that a mesh axis runs over, the one named last changes fastest.
Arguments:
- tokens: bfloat16 [32768, 2048], P('seq', 'tp'), may hold values from -6 to 6
- in_weight: bfloat16 [2048, 2, 2048], P(None, None, 'tp'), may hold values from -0.125 to 0.125
- bc_weight: bfloat16 [2048, 256], P(None, 'tp'), may hold values from -0.125 to 0.125
- dt_weight: bfloat16 [2, 2048, 32], P(None, None, 'tp'), may hold values from -0.125 to 0.125
- dt_bias: float32 [2, 32], P(None, 'tp'), may hold values from -2 to 0.5
- decay_rate: float32 [32], P('tp'), may hold values from 1e-05 to 0.5
- skip_gain: float32 [32], P('tp'), may hold values from 0.5 to 300
- out_weight: bfloat16 [2048, 2048], P('tp'), may hold values from -0.1875 to 0.1875
Outputs:
- mixed: bfloat16 [32768, 2048], P('seq', 'tp')
The draws below stay inside these ranges and needn't reach their ends.
All inputs are finite; a program needn't handle non-finite values.
Results may differ from the reference program's by a relative error of at most 0.018.
Values may be sent and summed in bfloat16 or wider, within the bound.
No kernel may reach another device: no remote copies, remote signals or barrier semaphores. Data moves between devices by JAX's collectives and lax.ppermute only.
A program may use at most 64 MiB of HBM per device.

```python
import math
import jax
import jax.numpy as jnp
from jax import lax

D = 2048
HEADS = 32
HEAD_DIM = 64
STATE = 128
TOK_DEV = 512
TOKENS = 32768
CHANNELS = 2048
N_SEQ = 64
N_TP = 8


def draw_decay_rate(key, part):
    key = jax.random.fold_in(key, 11)
    pick_key, slow_key, fast_key = jax.random.split(key, 3)
    share = 0.5
    slow_pick = jax.random.uniform(pick_key, (HEADS,), jnp.float32) < share
    slow_rate = jnp.exp(jax.random.uniform(slow_key, (HEADS,), jnp.float32, math.log(1e-05), math.log(0.0002)))
    fast_rate = jnp.exp(jax.random.uniform(fast_key, (HEADS,), jnp.float32, math.log(0.02), math.log(0.5)))
    return jnp.where(slow_pick, slow_rate, fast_rate).astype(jnp.float32)


def draw_skip_gain(key, part):
    key = jax.random.fold_in(key, 13)
    low_key = jax.random.fold_in(key, 1)
    gain = jnp.exp(jax.random.uniform(low_key, (HEADS,), jnp.float32, math.log(0.5), math.log(300.0)))
    return gain.astype(jnp.float32)


def with_spikes(drawn, key, source, target, parts, factor):
    def block_of(position):
        return (jnp.arange(drawn.shape[position]) // (drawn.shape[position] // parts)).reshape((-1,) + (1,) * (drawn.ndim - 1 - position))

    near = jax.random.permutation(key, parts)[block_of(target)]
    second = (block_of(target) + parts // 2) % parts
    return jnp.where((block_of(source) == near) | (block_of(source) == second), factor * drawn, drawn)


def steps_of(key, extent, cuts, least, top_value):
    def one(position, blocks):
        steps = jax.random.uniform(jax.random.fold_in(jax.random.fold_in(key, 6), position), (blocks,), jnp.float32, least / len(cuts), top_value / len(cuts))
        return jnp.repeat(jnp.exp(steps), extent[position] // blocks).reshape((-1,) + (1,) * (len(extent) - position - 1))

    level = one(*cuts[0])
    for cut in cuts[1:]:
        level = level * one(*cut)
    return level


def bell_draw(stream_key, shape, scale, bound, cuts=(), kind=jnp.bfloat16):
    factor_of = steps_of(stream_key, shape, cuts, -0.22, 0.18) if cuts else 1.0
    entries = jax.random.normal(stream_key, shape, jnp.float32) * scale * factor_of
    return jnp.minimum(jnp.maximum(entries, -bound), bound).astype(kind)


def bell_draw_with(own_key, extent, scale, limit, cuts, heavy, kind=jnp.bfloat16):
    drawn = scale * jax.random.normal(own_key, extent, jnp.float32)
    if cuts:
        drawn = drawn * steps_of(own_key, extent, cuts, -0.22, 0.18)
    return jnp.clip(with_spikes(drawn, jax.random.fold_in(own_key, 3), *heavy), -limit, limit).astype(kind)


def setup_inputs(seed: int = 0) -> dict:
    seeds = jax.random.split(jax.random.key(seed), 9)
    tokens = bell_draw(seeds[0], (TOKENS, D), 1.0, 6.0, ((0, 64), (1, 8)))
    in_weight = bell_draw(seeds[1], (D, 2, CHANNELS), D ** -0.5, 0.125, ((2, 8),))
    bc_weight = bell_draw(seeds[2], (D, 2 * STATE), D ** -0.5, 0.125, ((1, 8),))
    dt_weight = bell_draw(seeds[3], (2, D, HEADS), D ** -0.5, 0.125, ((2, 8),))
    dt_bias = jnp.clip(-2.0 + 2.5 * jax.random.uniform(seeds[4], (2, HEADS), jnp.float32) ** steps_of(seeds[4], (2, HEADS), ((1, 8),), -0.2, 0.2), -2.0, 0.5)
    decay_rate = draw_decay_rate(jax.random.fold_in(seeds[8], 71), 0)
    skip_gain = draw_skip_gain(jax.random.fold_in(seeds[8], 71), 0)
    out_weight = bell_draw_with(seeds[7], (CHANNELS, D), CHANNELS ** -0.5, 0.1875, ((0, 8),), (0, 1, 8, 2.0))
    return {"tokens": tokens, "in_weight": in_weight, "bc_weight": bc_weight, "dt_weight": dt_weight, "dt_bias": dt_bias, "decay_rate": decay_rate, "skip_gain": skip_gain, "out_weight": out_weight}


def block_terms(values, keys, queries, forward_steps, backward_steps, decay_rate):
    length = values.shape[0]
    forward_logs = -decay_rate[None, :] * forward_steps
    backward_logs = -decay_rate[None, :] * backward_steps
    forward_upto = jnp.cumsum(forward_logs, axis=0)
    forward_before = forward_upto - forward_logs
    backward_upto = jnp.cumsum(backward_logs, axis=0)
    backward_before = backward_upto - backward_logs
    forward_total = forward_upto[-1]
    backward_total = backward_upto[-1]
    scores = jnp.dot(queries, keys.T, preferred_element_type=jnp.float32)
    rows = jnp.arange(length, dtype=jnp.int32)[:, None]
    cols = jnp.arange(length, dtype=jnp.int32)[None, :]
    lower_mask = (rows > cols)[None]
    upper_mask = (rows < cols)[None]
    forward_gap = jnp.where(lower_mask, forward_before.T[:, :, None] - forward_upto.T[:, None, :], 0.0)
    forward_weights = jnp.where(lower_mask, scores[None] * jnp.exp(forward_gap) * forward_steps.T[:, None, :], 0.0).astype(jnp.bfloat16)
    backward_gap = jnp.where(upper_mask, backward_before.T[:, None, :] - backward_upto.T[:, :, None], 0.0)
    backward_weights = jnp.where(upper_mask, scores[None] * jnp.exp(backward_gap) * backward_steps.T[:, None, :], 0.0).astype(jnp.bfloat16)
    values_wide = values.astype(jnp.float32)
    inner = jnp.einsum('hts,shp->thp', forward_weights.astype(jnp.float32), values_wide)
    inner = inner + jnp.einsum('hts,shp->thp', backward_weights.astype(jnp.float32), values_wide)
    keys_wide = keys.astype(jnp.float32)
    forward_keys = (keys_wide[:, None, :] * (jnp.exp(forward_total[None, :] - forward_upto) * forward_steps)[:, :, None]).astype(jnp.bfloat16)
    backward_keys = (keys_wide[:, None, :] * (jnp.exp(backward_before) * backward_steps)[:, :, None]).astype(jnp.bfloat16)
    forward_state = jnp.einsum('shp,shn->hpn', values_wide, forward_keys.astype(jnp.float32))
    backward_state = jnp.einsum('shp,shn->hpn', values_wide, backward_keys.astype(jnp.float32))
    return (inner, forward_state, backward_state, forward_total, backward_total, forward_before, backward_upto)

def reference(tokens, in_weight, bc_weight, dt_weight, dt_bias, decay_rate, skip_gain, out_weight):
    tokens_wide = tokens.astype(jnp.float32)
    projected = jnp.einsum('td,dkf->tkf', tokens_wide, in_weight.astype(jnp.float32))
    values = projected[:, 0].astype(jnp.bfloat16).reshape(N_SEQ, TOK_DEV, HEADS, HEAD_DIM)
    gates = projected[:, 1].reshape(N_SEQ, TOK_DEV, HEADS, HEAD_DIM)
    both = jnp.dot(tokens, bc_weight, preferred_element_type=jnp.float32).astype(jnp.bfloat16)
    keys = both[:, :STATE].reshape(N_SEQ, TOK_DEV, STATE)
    queries = both[:, STATE:].reshape(N_SEQ, TOK_DEV, STATE)
    steps = jax.nn.softplus(jnp.einsum('td,kdh->kth', tokens_wide, dt_weight.astype(jnp.float32)) + dt_bias[:, None, :])
    forward_steps = steps[0].reshape(N_SEQ, TOK_DEV, HEADS)
    backward_steps = steps[1].reshape(N_SEQ, TOK_DEV, HEADS)
    results = lax.map(lambda items: block_terms(items[0], items[1], items[2], items[3], items[4], decay_rate), (values, keys, queries, forward_steps, backward_steps))
    inner, forward_state, backward_state, forward_total, backward_total, forward_before, backward_upto = results

    def carry_on(carry, items):
        state, total = items
        return (jnp.exp(total)[:, None, None] * carry + state, carry)
    zeros_state = jnp.zeros((HEADS, HEAD_DIM, STATE), jnp.float32)
    forward_enter = lax.scan(carry_on, zeros_state, (forward_state, forward_total))[1]
    backward_enter = lax.scan(carry_on, zeros_state, (backward_state, backward_total), reverse=True)[1]
    queries_wide = queries.astype(jnp.float32)
    mix = inner + jnp.exp(forward_before)[..., None] * jnp.einsum('btn,bhpn->bthp', queries_wide, forward_enter, precision=lax.Precision.HIGHEST)
    mix = mix + jnp.exp(backward_total[:, None, :] - backward_upto)[..., None] * jnp.einsum('btn,bhpn->bthp', queries_wide, backward_enter, precision=lax.Precision.HIGHEST)
    mix = mix + skip_gain[None, None, :, None] * values.astype(jnp.float32)
    gated = mix * jax.nn.silu(gates)
    power = lax.optimization_barrier(jnp.mean(gated * gated, axis=-1, keepdims=True))
    hidden = (gated * lax.rsqrt(power + 1e-05)).astype(jnp.bfloat16).reshape(TOKENS, CHANNELS)
    group = CHANNELS // N_TP

    def add_group(index, total):
        part_rows = lax.dynamic_slice_in_dim(hidden, (index * group).astype(jnp.int32), group, 1)
        part_weight = lax.dynamic_slice_in_dim(out_weight, (index * group).astype(jnp.int32), group, 0)
        rounded = jnp.dot(part_rows, part_weight, preferred_element_type=jnp.float32).astype(jnp.bfloat16)
        rounded = lax.optimization_barrier(rounded)
        return total + rounded.astype(jnp.float32)
    total = lax.fori_loop(0, N_TP, add_group, jnp.zeros((TOKENS, D), jnp.float32))
    return total.astype(jnp.bfloat16)
```

```python
import jax
import jax.numpy as jnp
from jax import lax
from jax.experimental import pallas as pl
from jax.experimental.pallas import tpu as pltpu
from jax.sharding import PartitionSpec as P

F32 = jnp.float32
BF16 = jnp.bfloat16
L = 512
D = 2048
W = 256
H = 4
HD = 64
N = 128
XS = 4
GROUP = 8
SLICE = N // GROUP

X_GROUPS = [[2 * x + c for x in range(XS)] for c in range(2)]
SWAP = [(i, i ^ 1) for i in range(8)]
NEAR = [[GROUP * g + j for j in range(GROUP)] for g in range(8)]
FAR = [[GROUP * g + j for g in range(8)] for j in range(GROUP)]

VMEM = pl.BlockSpec(memory_space=pltpu.VMEM)
SMEM = pl.BlockSpec(memory_space=pltpu.SMEM)
NN = (((1,), (0,)), ((), ()))
NT = (((1,), (1,)), ((), ()))


def dot(a, b, dims=NN):
    return lax.dot_general(a, b, dims, preferred_element_type=F32)


def iota(shape, axis):
    return lax.broadcasted_iota(jnp.int32, shape, axis)


def spread(width, base, copies):
    row = iota((N, width), 0)
    want = iota((N, width), 1) // HD + base
    hit = row == want
    for q in range(1, copies):
        hit = hit | (row == want + 8 * q)
    return hit.astype(BF16)


def widen(cols, base, width):
    pick = spread(width, base, 1)
    high = cols.astype(BF16)
    low = (cols - high.astype(F32)).astype(BF16)
    return dot(high, pick) + dot(low, pick)


def column(ref, rows):
    index = iota((2 * H, 1), 0)
    out = jnp.zeros((2 * H, 1), F32)
    for i in range(2 * H):
        out = jnp.where(index == i, rows(ref, i), out)
    return out


def project_kernel(
    core_ref, bias_ref, rate_ref, a_ref, b_ref, w_ref, d_ref,
    values_ref, gates_ref, query_ref, key_ref, rows_ref, cols_ref, message_ref,
):
    c = core_ref[0]
    tokens = []
    weights = []
    steps_weights = []
    bc_weights = []
    for x in range(XS):
        for ref, j in ((a_ref, 2 * x + c), (b_ref, 2 * x + 1 - c)):
            at = pl.multiple_of(j * W, W)
            tokens.append(ref[x, 0:L, :])
            weights.append(w_ref[pl.ds(at, W), :])
            steps_weights.append(d_ref[:, pl.ds(at, W)])
            row = pl.multiple_of(L + j * 32, 32)
            bc_weights.append(
                jnp.concatenate([r[y, pl.ds(row, 32), :] for y in range(XS) for r in (a_ref, b_ref)], axis=0)
            )
    whole = jnp.concatenate(tokens, axis=1)
    bc_weight = jnp.concatenate(bc_weights, axis=1)
    narrow = jnp.concatenate([bc_weight[:N], jnp.concatenate(steps_weights, axis=1)], axis=0)
    keys_steps = dot(narrow, whole, NT)
    key = keys_steps[:N].astype(BF16)
    key_ref[...] = key
    query_ref[...] = dot(whole, bc_weight[N:], NT).astype(BF16)
    both = dot(whole, jnp.concatenate(weights, axis=0))
    values = both[:, :W].astype(BF16)
    values_ref[...] = values
    gates_ref[...] = both[:, W:]

    raw = keys_steps[N : N + 2 * H] + column(bias_ref, lambda r, i: r[i // H, i % H])
    steps = jnp.maximum(raw, 0.0) + jnp.log1p(jnp.exp(-jnp.abs(raw)))
    logs = -column(rate_ref, lambda r, i: r[i % H]) * steps
    p1 = logs.astype(BF16)
    rest = logs - p1.astype(F32)
    p2 = rest.astype(BF16)
    p3 = (rest - p2.astype(F32)).astype(BF16)
    running = (iota((L, L), 0) <= iota((L, L), 1)).astype(BF16)
    parts = jnp.concatenate([p1.astype(F32), p2.astype(F32), p3.astype(F32), jnp.zeros((8, L), F32)], axis=0)
    summed = dot(parts.astype(BF16), running)
    upto = summed[0:8] + summed[8:16] + summed[16:24]
    before = upto - logs
    total = upto[:, L - 1 : L]
    forward = iota((2 * H, L), 0) < H
    scale = jnp.exp(jnp.where(forward, total - upto, before)) * steps
    reach = jnp.exp(jnp.where(forward, before, total - upto))
    rows = jnp.concatenate(
        [upto, upto, before, steps, scale, reach, jnp.zeros((N - 48, L), F32)], axis=0
    )
    rows_ref[...] = rows[0:48]
    cols = rows.T
    cols_ref[...] = cols

    wide = values.astype(F32)
    scaled = (jnp.concatenate([wide, wide], axis=1) * widen(cols, 32, 2 * W)).astype(BF16)
    state = dot(key, scaled).astype(BF16)
    last = cols[L - 1 : L, :]
    lane = iota((1, N), 1)
    high = last.astype(BF16).astype(F32)
    extra = jnp.where(lane < 8, high, jnp.where(lane < 16, last - high, 0.0))
    extra = jnp.broadcast_to(extra, (SLICE, N)).astype(BF16)
    for k in range(GROUP):
        message_ref[k, :, 0 : 2 * W] = state[SLICE * k : SLICE * (k + 1)]
        message_ref[k, :, 2 * W : 2 * W + N] = extra


def inner_kernel(skip_ref, query_ref, key_ref, values_ref, rows_ref, cols_ref, inner_ref):
    key = key_ref[...]
    values = values_ref[...]
    tile = 128
    lane = iota((tile, W), 1) // HD

    def body(i, carry):
        at = pl.ds(pl.multiple_of(i * tile, tile), tile)
        scores = dot(query_ref[at, :], key)
        t = iota((tile, L), 0) + i * tile
        s = iota((tile, L), 1)
        lower = s < t
        upper = s > t
        own = values_ref[at, :].astype(F32)
        gain = jnp.zeros((tile, W), F32)
        out = jnp.zeros((tile, W), F32)
        for h in range(H):
            gap = jnp.where(
                lower,
                cols_ref[at, 16 + h : 17 + h] - rows_ref[h : h + 1, :],
                rows_ref[20 + h : 21 + h, :] - cols_ref[at, H + h : H + h + 1],
            )
            step = jnp.where(lower, rows_ref[24 + h : 25 + h, :], rows_ref[28 + h : 29 + h, :])
            weight = jnp.where(lower | upper, scores * jnp.exp(gap) * step, 0.0).astype(BF16)
            out = jnp.where(lane == h, dot(weight, values), out)
            gain = jnp.where(lane == h, skip_ref[h], gain)
        inner_ref[at, :] = out + gain * own
        return carry

    lax.fori_loop(0, L // tile, body, 0)


def near_states(got_ref):
    extra = got_ref[:, :, 2 * W : 2 * W + N].reshape(GROUP * SLICE, N)
    decay = jnp.exp(dot(extra, spread(2 * W, 0, 2)))
    states = [got_ref[j, :, 0 : 2 * W].astype(F32) for j in range(GROUP)]
    decays = [decay[SLICE * j : SLICE * (j + 1)] for j in range(GROUP)]
    return states, decays


def totals_kernel(group_ref, got_ref, out_ref):
    g = group_ref[0]
    states, decays = near_states(got_ref)
    forward = states[0][:, :W]
    for j in range(1, GROUP):
        forward = decays[j][:, :W] * forward + states[j][:, :W]
    backward = states[GROUP - 1][:, W:]
    for j in range(GROUP - 2, -1, -1):
        backward = decays[j][:, W:] * backward + states[j][:, W:]
    log = jnp.zeros((SLICE, N), F32)
    for j in range(GROUP):
        log = log + got_ref[j, :, 2 * W : 2 * W + N].astype(F32)
    high = log.astype(BF16).astype(F32)
    log = (high + pltpu.roll(log - high, 16, 1)).astype(BF16)
    forward = forward.astype(BF16)
    backward = backward.astype(BF16)
    for q in range(8):
        out_ref[q, :, 0:W] = jnp.where(q > g, forward, backward)
        out_ref[q, :, W : W + N] = log


def enter_kernel(group_ref, got_ref, far_ref, out_ref):
    g = group_ref[0]
    states, decays = near_states(got_ref)
    extra = far_ref[:, :, W : W + N].reshape(8 * SLICE, N)
    decay = jnp.exp(dot(extra, spread(2 * W, 0, 4)))
    forward = jnp.zeros((SLICE, W), F32)
    backward = jnp.zeros((SLICE, W), F32)
    for q in range(8):
        rows = slice(SLICE * q, SLICE * (q + 1))
        forward = jnp.where(q < g, decay[rows, :W] * forward + far_ref[q, :, 0:W].astype(F32), forward)
    for q in range(7, -1, -1):
        rows = slice(SLICE * q, SLICE * (q + 1))
        backward = jnp.where(q > g, decay[rows, W:] * backward + far_ref[q, :, 0:W].astype(F32), backward)
    for j in range(GROUP):
        out_ref[j, :, 0:W] = forward.astype(BF16)
        forward = decays[j][:, :W] * forward + states[j][:, :W]
    for j in range(GROUP - 1, -1, -1):
        out_ref[j, :, W : 2 * W] = backward.astype(BF16)
        backward = decays[j][:, W:] * backward + states[j][:, W:]


def mix_kernel(core_ref, inner_ref, gates_ref, query_ref, enter_ref, cols_ref, w_ref, hidden_ref, part_ref):
    carried = dot(query_ref[...], enter_ref[...]) * widen(cols_ref[...], 40, 2 * W)
    mix = inner_ref[...] + carried[:, :W] + carried[:, W:]
    gates = gates_ref[...]
    gated = mix * (gates / (1.0 + jnp.exp(-gates)))
    square = gated * gated
    same = (iota((W, W), 0) // HD == iota((W, W), 1) // HD).astype(BF16)
    high = square.astype(BF16)
    low = (square - high.astype(F32)).astype(BF16)
    power = (dot(high, same) + dot(low, same)) * (1.0 / HD)
    hidden = (gated * lax.rsqrt(power + 1e-05)).astype(BF16)
    hidden_ref[...] = hidden
    other = 1 - core_ref[0]
    for x in range(XS):
        at = pl.multiple_of((2 * x + other) * W, W)
        part_ref[x] = dot(hidden, w_ref[:, pl.ds(at, W)]).astype(BF16)


def pair_kernel(core_ref, hidden_ref, w_ref, got_ref, out_ref):
    hidden = hidden_ref[...]
    for x in range(XS):
        at = pl.multiple_of((2 * x + core_ref[0]) * W, W)
        out_ref[x] = (dot(hidden, w_ref[:, pl.ds(at, W)]) + got_ref[x].astype(F32)).astype(BF16)


def call(kernel, name, ins, outs, flops, *operands):
    return pl.pallas_call(
        kernel,
        name=name,
        in_specs=ins,
        out_specs=[VMEM] * len(outs),
        out_shape=[jax.ShapeDtypeStruct(shape, kind) for shape, kind in outs],
        compiler_params=pltpu.CompilerParams(vmem_limit_bytes=48 << 20),
        cost_estimate=pl.CostEstimate(flops=flops, bytes_accessed=1 << 21, transcendentals=1 << 16),
    )(*operands)


def shards(tokens, in_weight, bc_weight, dt_weight, dt_bias, decay_rate, skip_gain, out_weight):
    core = (lax.axis_index("tp") % 2).astype(jnp.int32)[None]
    group = (lax.axis_index("seq") // GROUP).astype(jnp.int32)[None]
    bc_rows = bc_weight.T.reshape(32, 8, W).transpose(1, 0, 2).reshape(8 * 32, W)
    payload = jnp.concatenate([tokens, bc_rows], axis=0)
    payload = jnp.broadcast_to(payload[None], (XS, L + W, W))
    mine = lax.all_to_all(payload, "tp", 0, 0, axis_index_groups=X_GROUPS, tiled=True)
    theirs = lax.ppermute(mine, "tp", SWAP)
    flat_weight = in_weight.reshape(D, 2 * W)
    steps_weight = jnp.pad(dt_weight.transpose(0, 2, 1).reshape(2 * H, D), ((0, 8), (0, 0)))
    values, gates, query, key, rows, cols, message = call(
        project_kernel,
        "project",
        [SMEM, SMEM, SMEM, VMEM, VMEM, VMEM, VMEM],
        [
            ((L, W), BF16),
            ((L, W), F32),
            ((L, N), BF16),
            ((N, L), BF16),
            ((48, L), F32),
            ((L, N), F32),
            ((GROUP, SLICE, 2 * W + N), BF16),
        ],
        1 << 31,
        core, dt_bias, decay_rate, mine, theirs, flat_weight, steps_weight,
    )
    near = lax.all_to_all(message, "seq", 0, 0, axis_index_groups=NEAR, tiled=True)
    (inner,) = call(
        inner_kernel,
        "inside",
        [SMEM, VMEM, VMEM, VMEM, VMEM, VMEM],
        [((L, W), F32)],
        1 << 31,
        skip_gain, query, key, values, rows, cols,
    )
    (totals,) = call(
        totals_kernel, "totals", [SMEM, VMEM], [((8, SLICE, W + N), BF16)], 1 << 20, group, near
    )
    far = lax.all_to_all(totals, "seq", 0, 0, axis_index_groups=FAR, tiled=True)
    (enters,) = call(
        enter_kernel, "enters", [SMEM, VMEM, VMEM], [((GROUP, SLICE, 2 * W), BF16)], 1 << 20, group, near, far
    )
    enter = lax.all_to_all(enters, "seq", 0, 0, axis_index_groups=NEAR, tiled=True).reshape(N, 2 * W)
    hidden, part = call(
        mix_kernel,
        "mix",
        [SMEM, VMEM, VMEM, VMEM, VMEM, VMEM, VMEM],
        [((L, W), BF16), ((XS, L, W), BF16)],
        1 << 29,
        core, inner, gates, query, enter, cols, out_weight,
    )
    got = lax.ppermute(part, "tp", SWAP)
    (paired,) = call(
        pair_kernel, "pair", [SMEM, VMEM, VMEM, VMEM], [((XS, L, W), BF16)], 1 << 28, core, hidden, out_weight, got
    )
    pieces = lax.all_to_all(paired, "tp", 0, 0, axis_index_groups=X_GROUPS, tiled=True)
    return jnp.sum(pieces.astype(F32), axis=0).astype(BF16)


def solution(mesh):
    in_specs = (
        P("seq", "tp"),
        P(None, None, "tp"),
        P(None, "tp"),
        P(None, None, "tp"),
        P(None, "tp"),
        P("tp"),
        P("tp"),
        P("tp", None),
    )
    out_specs = P("seq", "tp")
    return jax.shard_map(shards, mesh=mesh, in_specs=in_specs, out_specs=out_specs, check_vma=False)
```

```python
import jax
import jax.numpy as jnp
from jax import lax
from jax.experimental import pallas as pl
from jax.experimental.pallas import tpu as pltpu
from jax.sharding import PartitionSpec as P

F32 = jnp.float32
BF16 = jnp.bfloat16
L = 512
D = 2048
W = 256
H = 4
HD = 64
N = 128
XS = 4
GROUP = 8
SLICE = N // GROUP

X_GROUPS = [[2 * x + c for x in range(XS)] for c in range(2)]
PAIRS = [[2 * x, 2 * x + 1] for x in range(XS)]
SWAP = [(i, i ^ 1) for i in range(8)]
NEAR = [[GROUP * g + j for j in range(GROUP)] for g in range(8)]
FAR = [[GROUP * g + j for g in range(8)] for j in range(GROUP)]

VMEM = pl.BlockSpec(memory_space=pltpu.VMEM)
SMEM = pl.BlockSpec(memory_space=pltpu.SMEM)
HBM = pl.BlockSpec(memory_space=pltpu.HBM)
NN = (((1,), (0,)), ((), ()))
NT = (((1,), (1,)), ((), ()))


def dot(a, b, dims=NN):
    return lax.dot_general(a, b, dims, preferred_element_type=F32)


def iota(shape, axis):
    return lax.broadcasted_iota(jnp.int32, shape, axis)


def spread(width, base, copies):
    row = iota((N, width), 0)
    want = iota((N, width), 1) // HD + base
    hit = row == want
    for q in range(1, copies):
        hit = hit | (row == want + 8 * q)
    return hit.astype(BF16)


def widen(cols, base, width):
    pick = spread(width, base, 1)
    high = cols.astype(BF16)
    low = (cols - high.astype(F32)).astype(BF16)
    return dot(high, pick) + dot(low, pick)


def column(ref, rows):
    index = iota((2 * H, 1), 0)
    out = jnp.zeros((2 * H, 1), F32)
    for i in range(2 * H):
        out = jnp.where(index == i, rows(ref, i), out)
    return out


def prep_kernel(tokens_ref, bc_ref, out_ref, sems):
    copies = []
    for x in range(XS):
        copies.append(pltpu.make_async_copy(tokens_ref, out_ref.at[x, pl.ds(0, L)], sems.at[len(copies)]))
        for b in range(8):
            copies.append(
                pltpu.make_async_copy(
                    bc_ref.at[:, pl.ds(W * b, W)], out_ref.at[x, pl.ds(L + 32 * b, 32)], sems.at[len(copies)]
                )
            )
    for copy in copies:
        copy.start()
    for copy in copies:
        copy.wait()


def columns_kernel(core_ref, w_ref, out_ref):
    for x in range(XS):
        at = pl.multiple_of((2 * x + 1 - core_ref[0]) * W, W)
        out_ref[:, W * x : W * (x + 1)] = w_ref[:, pl.ds(at, W)]


def bc_columns(ref, first, j):
    row = pl.multiple_of(L + j * 32, 32)
    return [ref[x, pl.ds(row, 32), :] for x in (first, first + 1)]


def wide_part(ref, w_ref, c):
    total = None
    for x in range(XS):
        rows = pl.ds(pl.multiple_of((2 * x + c) * W, W), W)
        term = dot(ref[x, 0:L, :], w_ref[rows, :])
        total = term if total is None else total + term
    return total


def narrow_part(ref, refs, d_ref, c):
    total = None
    for x in range(XS):
        j = 2 * x + c
        pieces = [piece for r in refs for piece in bc_columns(r, 0, j)]
        if d_ref is not None:
            pieces.append(d_ref[:, pl.ds(pl.multiple_of(j * W, W), W)])
        term = dot(jnp.concatenate(pieces, axis=0), ref[x, 0:L, :], NT)
        total = term if total is None else total + term
    return total


def query_part(ref, refs, c):
    total = None
    for x in range(XS):
        pieces = [piece for r in refs for piece in bc_columns(r, 2, 2 * x + c)]
        term = dot(ref[x, 0:L, :], jnp.concatenate(pieces, axis=0), NT)
        total = term if total is None else total + term
    return total


def half_kernel(core_ref, a_ref, w_ref, d_ref, wide_ref, narrow_ref, steps_ref, high_ref):
    c = core_ref[0]
    high_ref[...] = jnp.zeros((SLICE, D), F32)
    for i in range(2):
        high_ref[H * i : H * (i + 1), :] = d_ref[i].astype(F32)
    steps_ref[...] = high_ref[...].astype(BF16)
    wide_ref[...] = wide_part(a_ref, w_ref, c)
    narrow_ref[...] = narrow_part(a_ref, (a_ref,), steps_ref, c)


def project_kernel(
    core_ref, bias_ref, rate_ref, a_ref, b_ref, w_ref, d_ref, half_ref, narrow_ref,
    values_ref, gates_ref, query_ref, key_ref, rows_ref, message_ref,
):
    c = core_ref[0]
    later = narrow_part(b_ref, (a_ref, b_ref), d_ref, 1 - c)
    earlier = narrow_ref[...]
    key = jnp.concatenate(
        [earlier[0:64] + later[0:64], narrow_part(a_ref, (b_ref,), None, c) + later[64:128]], axis=0
    ).astype(BF16)
    key_ref[...] = key
    both = half_ref[...] + wide_part(b_ref, w_ref, 1 - c)
    values = both[:, :W].astype(BF16)
    values_ref[...] = values
    gates_ref[...] = both[:, W:]
    query_ref[...] = (query_part(a_ref, (a_ref, b_ref), c) + query_part(b_ref, (a_ref, b_ref), 1 - c)).astype(BF16)
    raw = (earlier[64:72] + later[128:136]) + column(bias_ref, lambda r, i: r[i // H, i % H])
    steps = jnp.maximum(raw, 0.0) + jnp.log1p(jnp.exp(-jnp.abs(raw)))
    logs = -column(rate_ref, lambda r, i: r[i % H]) * steps
    p1 = logs.astype(BF16)
    rest = logs - p1.astype(F32)
    p2 = rest.astype(BF16)
    p3 = (rest - p2.astype(F32)).astype(BF16)
    running = (iota((L, L), 0) <= iota((L, L), 1)).astype(BF16)
    parts = jnp.concatenate([p1.astype(F32), p2.astype(F32), p3.astype(F32), jnp.zeros((8, L), F32)], axis=0)
    summed = dot(parts.astype(BF16), running)
    upto = summed[0:8] + summed[8:16] + summed[16:24]
    before = upto - logs
    total = upto[:, L - 1 : L]
    forward = iota((2 * H, L), 0) < H
    scale = jnp.exp(jnp.where(forward, total - upto, before)) * steps
    reach = jnp.exp(jnp.where(forward, before, total - upto))
    rows_ref[...] = jnp.concatenate([upto, before, steps, reach], axis=0)

    wide = key.astype(F32)
    scaled = jnp.concatenate([(wide * scale[i : i + 1]).astype(BF16) for i in range(2 * H)], axis=0)
    state = dot(scaled, values)
    head = iota((N, W), 1) // HD
    sides = []
    for first in (0, H):
        out = state[N * first : N * (first + 1)]
        for h in range(1, H):
            out = jnp.where(head == h, state[N * (first + h) : N * (first + h + 1)], out)
        sides.append(out.astype(BF16))
    lane = iota((2 * H, N), 1)
    mine_only = (iota((2 * H, N), 0) == lane % 8) & (lane < 16)
    last = jnp.sum(jnp.where(mine_only, total, 0.0), axis=0, keepdims=True)
    high = last.astype(BF16).astype(F32)
    extra = jnp.where(iota((1, N), 1) < 8, high, last - high)
    extra = jnp.broadcast_to(extra, (SLICE, N)).astype(BF16)
    for k in range(GROUP):
        for i in range(2):
            message_ref[k, :, W * i : W * (i + 1)] = sides[i][SLICE * k : SLICE * (k + 1)]
        message_ref[k, :, 2 * W : 2 * W + N] = extra


def inner_kernel(skip_ref, query_ref, key_ref, values_ref, rows_ref, inner_ref, cols_ref):
    cols_ref[...] = jnp.concatenate([rows_ref[...], jnp.zeros((N - 32, L), F32)], axis=0).T
    key = key_ref[...]
    values = values_ref[...]
    tile = 128
    lane = iota((tile, W), 1) // HD

    def body(i, carry):
        at = pl.ds(pl.multiple_of(i * tile, tile), tile)
        scores = dot(query_ref[at, :], key)
        t = iota((tile, L), 0) + i * tile
        s = iota((tile, L), 1)
        lower = s < t
        upper = s > t
        own = values_ref[at, :].astype(F32)
        gain = jnp.zeros((tile, W), F32)
        out = jnp.zeros((tile, W), F32)
        for h in range(H):
            gap = jnp.where(
                lower,
                cols_ref[at, 8 + h : 9 + h] - rows_ref[h : h + 1, :],
                rows_ref[12 + h : 13 + h, :] - cols_ref[at, H + h : H + h + 1],
            )
            step = jnp.where(lower, rows_ref[16 + h : 17 + h, :], rows_ref[20 + h : 21 + h, :])
            weight = jnp.where(lower | upper, scores * jnp.exp(gap) * step, 0.0).astype(BF16)
            out = jnp.where(lane == h, dot(weight, values), out)
            gain = jnp.where(lane == h, skip_ref[h], gain)
        inner_ref[at, :] = out + gain * own
        return carry

    lax.fori_loop(0, L // tile, body, 0)


def near_states(got_ref):
    extra = got_ref[:, :, 2 * W : 2 * W + N].reshape(GROUP * SLICE, N)
    decay = jnp.exp(dot(extra, spread(2 * W, 0, 2)))
    states = [got_ref[j, :, 0 : 2 * W].astype(F32) for j in range(GROUP)]
    decays = [decay[SLICE * j : SLICE * (j + 1)] for j in range(GROUP)]
    return states, decays


def totals_kernel(group_ref, got_ref, out_ref):
    g = group_ref[0]
    states, decays = near_states(got_ref)
    forward = states[0][:, :W]
    for j in range(1, GROUP):
        forward = decays[j][:, :W] * forward + states[j][:, :W]
    backward = states[GROUP - 1][:, W:]
    for j in range(GROUP - 2, -1, -1):
        backward = decays[j][:, W:] * backward + states[j][:, W:]
    log = jnp.zeros((SLICE, N), F32)
    for j in range(GROUP):
        log = log + got_ref[j, :, 2 * W : 2 * W + N].astype(F32)
    high = log.astype(BF16).astype(F32)
    log = (high + pltpu.roll(log - high, 16, 1)).astype(BF16)
    forward = forward.astype(BF16)
    backward = backward.astype(BF16)
    for q in range(8):
        out_ref[q, :, 0:W] = jnp.where(q > g, forward, backward)
        out_ref[q, :, W : W + N] = log


def enter_kernel(group_ref, got_ref, far_ref, out_ref):
    g = group_ref[0]
    states, decays = near_states(got_ref)
    extra = far_ref[:, :, W : W + N].reshape(8 * SLICE, N)
    decay = jnp.exp(dot(extra, spread(2 * W, 0, 4)))
    forward = jnp.zeros((SLICE, W), F32)
    backward = jnp.zeros((SLICE, W), F32)
    for q in range(8):
        rows = slice(SLICE * q, SLICE * (q + 1))
        forward = jnp.where(q < g, decay[rows, :W] * forward + far_ref[q, :, 0:W].astype(F32), forward)
    for q in range(7, -1, -1):
        rows = slice(SLICE * q, SLICE * (q + 1))
        backward = jnp.where(q > g, decay[rows, W:] * backward + far_ref[q, :, 0:W].astype(F32), backward)
    for j in range(GROUP):
        out_ref[j, :, 0:W] = forward.astype(BF16)
        forward = decays[j][:, :W] * forward + states[j][:, :W]
    for j in range(GROUP - 1, -1, -1):
        out_ref[j, :, W : 2 * W] = backward.astype(BF16)
        backward = decays[j][:, W:] * backward + states[j][:, W:]


def mix_kernel(inner_ref, gates_ref, query_ref, enter_ref, cols_ref, hidden_ref):
    carried = dot(query_ref[...], enter_ref[...]) * widen(cols_ref[...], 24, 2 * W)
    mix = inner_ref[...] + carried[:, :W] + carried[:, W:]
    gates = gates_ref[...]
    gated = mix * (gates / (1.0 + jnp.exp(-gates)))
    square = gated * gated
    same = (iota((W, W), 0) // HD == iota((W, W), 1) // HD).astype(BF16)
    high = square.astype(BF16)
    low = (square - high.astype(F32)).astype(BF16)
    power = (dot(high, same) + dot(low, same)) * (1.0 / HD)
    hidden_ref[...] = (gated * lax.rsqrt(power + 1e-05)).astype(BF16)


def pair_kernel(core_ref, hidden_ref, w_ref, other_ref, out_ref):
    c = core_ref[0]
    hidden = jnp.concatenate([hidden_ref[c], hidden_ref[1 - c]], axis=1)
    for x in range(XS):
        at = pl.ds(pl.multiple_of((2 * x + c) * W, W), W)
        out_ref[x] = dot(hidden, jnp.concatenate([w_ref[:, at], other_ref[:, W * x : W * (x + 1)]], axis=0)).astype(BF16)


def sum_kernel(pieces_ref, out_ref):
    total = pieces_ref[0].astype(F32) + pieces_ref[1].astype(F32)
    total = total + pieces_ref[2].astype(F32) + pieces_ref[3].astype(F32)
    out_ref[...] = total.astype(BF16)


def call(kernel, name, ins, outs, flops, *operands, touched=1 << 21, scratch=(), out_spec=VMEM):
    return pl.pallas_call(
        kernel,
        name=name,
        in_specs=ins,
        out_specs=[out_spec] * len(outs),
        scratch_shapes=scratch,
        out_shape=[jax.ShapeDtypeStruct(shape, kind) for shape, kind in outs],
        compiler_params=pltpu.CompilerParams(vmem_limit_bytes=20 << 20),
        cost_estimate=pl.CostEstimate(flops=flops, bytes_accessed=touched, transcendentals=1 << 16),
    )(*operands)


def shards(tokens, in_weight, bc_weight, dt_weight, dt_bias, decay_rate, skip_gain, out_weight):
    core = (lax.axis_index("tp").astype(jnp.int32) & 1)[None]
    group = (lax.axis_index("seq").astype(jnp.int32) >> 3)[None]
    (payload,) = call(
        prep_kernel,
        "payload",
        [HBM, HBM],
        [((XS, L + W, W), BF16)],
        1,
        tokens,
        bc_weight.T,
        touched=0,
        scratch=[pltpu.SemaphoreType.DMA((9 * XS,))],
        out_spec=HBM,
    )
    flat_weight = in_weight.reshape(D, 2 * W)
    steps_weight = dt_weight.transpose(0, 2, 1)
    mine = lax.all_to_all(payload, "tp", 0, 0, axis_index_groups=X_GROUPS, tiled=True)
    (other_weight,) = call(
        columns_kernel, "columns", [SMEM, VMEM], [((W, XS * W), BF16)], 1, core, out_weight
    )
    other_weight = lax.ppermute(other_weight, "tp", SWAP)
    mine, core, group, other_weight = lax.optimization_barrier((mine, core, group, other_weight))
    theirs = lax.ppermute(mine, "tp", SWAP)
    half, narrow, steps_weight = call(
        half_kernel,
        "half",
        [SMEM, VMEM, VMEM, VMEM],
        [((L, 2 * W), F32), ((80, L), F32), ((SLICE, D), BF16)],
        1 << 30,
        core, mine, flat_weight, steps_weight,
        scratch=[pltpu.VMEM((SLICE, D), F32)],
    )
    values, gates, query, key, rows, message = call(
        project_kernel,
        "project",
        [SMEM, SMEM, SMEM, VMEM, VMEM, VMEM, VMEM, VMEM, VMEM],
        [
            ((L, W), BF16),
            ((L, W), F32),
            ((L, N), BF16),
            ((N, L), BF16),
            ((32, L), F32),
            ((GROUP, SLICE, 2 * W + N), BF16),
        ],
        1 << 31,
        core, dt_bias, decay_rate, mine, theirs, flat_weight, steps_weight, half, narrow,
    )
    near = lax.all_to_all(message, "seq", 0, 0, axis_index_groups=NEAR, tiled=True)
    inner, cols = call(
        inner_kernel,
        "inside",
        [SMEM, VMEM, VMEM, VMEM, VMEM],
        [((L, W), F32), ((L, N), F32)],
        1 << 31,
        skip_gain, query, key, values, rows,
    )
    (totals,) = call(
        totals_kernel, "totals", [SMEM, VMEM], [((8, SLICE, W + N), BF16)], 1 << 20, group, near
    )
    far = lax.all_to_all(totals, "seq", 0, 0, axis_index_groups=FAR, tiled=True)
    far, inner, cols = lax.optimization_barrier((far, inner, cols))
    (enters,) = call(
        enter_kernel, "enters", [SMEM, VMEM, VMEM], [((GROUP, SLICE, 2 * W), BF16)], 1 << 20, group, near, far
    )
    enter = lax.all_to_all(enters, "seq", 0, 0, axis_index_groups=NEAR, tiled=True).reshape(N, 2 * W)
    (hidden,) = call(
        mix_kernel, "mix", [VMEM] * 5, [((L, W), BF16)], 1 << 28, inner, gates, query, enter, cols
    )
    hidden = lax.all_gather(hidden, "tp", axis_index_groups=PAIRS)
    (paired,) = call(
        pair_kernel, "pair", [SMEM, VMEM, VMEM, VMEM], [((XS, L, W), BF16)], 1 << 29, core, hidden, out_weight, other_weight
    )
    pieces = lax.all_to_all(paired, "tp", 0, 0, axis_index_groups=X_GROUPS, tiled=True)
    return call(sum_kernel, "sum", [VMEM], [((L, W), BF16)], 1 << 20, pieces)[0]


def solution(mesh):
    in_specs = (
        P("seq", "tp"),
        P(None, None, "tp"),
        P(None, "tp"),
        P(None, None, "tp"),
        P(None, "tp"),
        P("tp"),
        P("tp"),
        P("tp", None),
    )
    out_specs = P("seq", "tp")
    return jax.shard_map(shards, mesh=mesh, in_specs=in_specs, out_specs=out_specs, check_vma=False)
```

```python
import jax
import jax.numpy as jnp
from jax import lax
from jax.experimental import pallas as pl
from jax.experimental.pallas import tpu as pltpu
from jax.sharding import PartitionSpec as P

F32 = jnp.float32
BF16 = jnp.bfloat16
L = 512
D = 2048
W = 256
H = 4
HD = 64
N = 128
XS = 4
GROUP = 8
SLICE = N // GROUP

X_ORDER = [3, 2, 1, 0]
X_GROUPS = [[2 * x + c for x in X_ORDER] for c in range(2)]
PAIRS = [[2 * x, 2 * x + 1] for x in range(XS)]
SWAP = [(i, i ^ 1) for i in range(8)]
NEAR_ORDER = [7, 6, 5, 4, 3, 2, 1, 0]
NEAR = [[GROUP * g + j for j in NEAR_ORDER] for g in range(8)]
FAR_ORDER = [4, 5, 6, 7, 3, 2, 1, 0]
FAR = [[GROUP * g + j for g in FAR_ORDER] for j in range(GROUP)]

VMEM = pl.BlockSpec(memory_space=pltpu.VMEM)
SMEM = pl.BlockSpec(memory_space=pltpu.SMEM)
HBM = pl.BlockSpec(memory_space=pltpu.HBM)
NN = (((1,), (0,)), ((), ()))
NT = (((1,), (1,)), ((), ()))


def dot(a, b, dims=NN):
    return lax.dot_general(a, b, dims, preferred_element_type=F32)


def iota(shape, axis):
    return lax.broadcasted_iota(jnp.int32, shape, axis)


def spread(width, base, copies):
    row = iota((N, width), 0)
    want = iota((N, width), 1) // HD + base
    hit = row == want
    for q in range(1, copies):
        hit = hit | (row == want + 8 * q)
    return hit.astype(BF16)


def widen(cols, base, width):
    pick = spread(width, base, 1)
    high = cols.astype(BF16)
    low = (cols - high.astype(F32)).astype(BF16)
    return dot(high, pick) + dot(low, pick)


def column(ref, rows):
    index = iota((2 * H, 1), 0)
    out = jnp.zeros((2 * H, 1), F32)
    for i in range(2 * H):
        out = jnp.where(index == i, rows(ref, i), out)
    return out


def prep_kernel(tokens_ref, bc_ref, out_ref, rows_ref, sems):
    copies = []
    for x in range(XS):
        copies.append(pltpu.make_async_copy(tokens_ref, out_ref.at[x, pl.ds(0, L)], sems.at[x]))
        copies[-1].start()
    for b in range(8):
        rows_ref[32 * b : 32 * (b + 1), :] = bc_ref[:, W * b : W * (b + 1)]
    for x in range(XS):
        copies.append(pltpu.make_async_copy(rows_ref, out_ref.at[x, pl.ds(L, W)], sems.at[XS + x]))
        copies[-1].start()
    for copy in copies:
        copy.wait()


def columns_kernel(core_ref, w_ref, own_ref, out_ref):
    for x in range(XS):
        for ref, c in ((own_ref, core_ref[0]), (out_ref, 1 - core_ref[0])):
            ref[:, W * x : W * (x + 1)] = w_ref[:, pl.ds(pl.multiple_of((2 * x + c) * W, W), W)]


def bc_columns(ref, first, j):
    row = pl.multiple_of(L + j * 32, 32)
    return [ref[X_ORDER.index(x), pl.ds(row, 32), :] for x in (first, first + 1)]


def wide_part(ref, w_ref, c):
    total = None
    for x in range(XS):
        rows = pl.ds(pl.multiple_of((2 * x + c) * W, W), W)
        term = dot(ref[X_ORDER.index(x), 0:L, :], w_ref[rows, :])
        total = term if total is None else total + term
    return total


def narrow_part(ref, refs, d_ref, c):
    total = None
    for x in range(XS):
        j = 2 * x + c
        pieces = [piece for r in refs for piece in bc_columns(r, 0, j)]
        if d_ref is not None:
            pieces.append(d_ref[:, pl.ds(pl.multiple_of(j * W, W), W)])
        term = dot(jnp.concatenate(pieces, axis=0), ref[X_ORDER.index(x), 0:L, :], NT)
        total = term if total is None else total + term
    return total


def query_part(ref, refs, c):
    total = None
    for x in range(XS):
        pieces = [piece for r in refs for piece in bc_columns(r, 2, 2 * x + c)]
        term = dot(ref[X_ORDER.index(x), 0:L, :], jnp.concatenate(pieces, axis=0), NT)
        total = term if total is None else total + term
    return total


def half_kernel(core_ref, a_ref, w_ref, d_ref, wide_ref, narrow_ref, steps_ref, high_ref):
    c = core_ref[0]
    high_ref[...] = jnp.zeros((SLICE, D), F32)
    for i in range(2):
        high_ref[H * i : H * (i + 1), :] = d_ref[i].astype(F32)
    steps_ref[...] = high_ref[...].astype(BF16)
    wide_ref[...] = wide_part(a_ref, w_ref, c)
    narrow_ref[...] = narrow_part(a_ref, (a_ref,), steps_ref, c)


def project_kernel(
    core_ref, bias_ref, rate_ref, a_ref, b_ref, w_ref, d_ref, half_ref, narrow_ref,
    values_ref, gates_ref, query_ref, key_ref, rows_ref, message_ref,
):
    c = core_ref[0]
    later = narrow_part(b_ref, (a_ref, b_ref), d_ref, 1 - c)
    earlier = narrow_ref[...]
    key = jnp.concatenate(
        [earlier[0:64] + later[0:64], narrow_part(a_ref, (b_ref,), None, c) + later[64:128]], axis=0
    ).astype(BF16)
    key_ref[...] = key
    both = half_ref[...] + wide_part(b_ref, w_ref, 1 - c)
    values = both[:, :W].astype(BF16)
    values_ref[...] = values
    gates_ref[...] = both[:, W:]
    query_ref[...] = (query_part(a_ref, (a_ref, b_ref), c) + query_part(b_ref, (a_ref, b_ref), 1 - c)).astype(BF16)
    raw = (earlier[64:72] + later[128:136]) + column(bias_ref, lambda r, i: r[i // H, i % H])
    steps = jnp.maximum(raw, 0.0) + jnp.log1p(jnp.exp(-jnp.abs(raw)))
    logs = -column(rate_ref, lambda r, i: r[i % H]) * steps
    p1 = logs.astype(BF16)
    rest = logs - p1.astype(F32)
    p2 = rest.astype(BF16)
    p3 = (rest - p2.astype(F32)).astype(BF16)
    running = (iota((L, L), 0) <= iota((L, L), 1)).astype(BF16)
    parts = jnp.concatenate([p1.astype(F32), p2.astype(F32), p3.astype(F32), jnp.zeros((8, L), F32)], axis=0)
    summed = dot(parts.astype(BF16), running)
    upto = summed[0:8] + summed[8:16] + summed[16:24]
    before = upto - logs
    total = upto[:, L - 1 : L]
    forward = iota((2 * H, L), 0) < H
    scale = jnp.exp(jnp.where(forward, total - upto, before)) * steps
    reach = jnp.exp(jnp.where(forward, before, total - upto))
    rows_ref[...] = jnp.concatenate([upto, before, steps, reach], axis=0)

    wide = key.astype(F32)
    scaled = jnp.concatenate([(wide * scale[i : i + 1]).astype(BF16) for i in range(2 * H)], axis=0)
    state = dot(scaled, values)
    head = iota((N, W), 1) // HD
    sides = []
    for first in (0, H):
        out = state[N * first : N * (first + 1)]
        for h in range(1, H):
            out = jnp.where(head == h, state[N * (first + h) : N * (first + h + 1)], out)
        sides.append(out.astype(BF16))
    lane = iota((2 * H, N), 1)
    mine_only = (iota((2 * H, N), 0) == lane % 8) & (lane < 16)
    last = jnp.sum(jnp.where(mine_only, total, 0.0), axis=0, keepdims=True)
    high = last.astype(BF16).astype(F32)
    extra = jnp.where(iota((1, N), 1) < 8, high, last - high)
    extra = jnp.broadcast_to(extra, (SLICE, N)).astype(BF16)
    for k in range(GROUP):
        for i in range(2):
            message_ref[k, :, W * i : W * (i + 1)] = sides[i][SLICE * k : SLICE * (k + 1)]
        message_ref[k, :, 2 * W : 2 * W + N] = extra


def inner_kernel(skip_ref, query_ref, key_ref, values_ref, rows_ref, inner_ref, cols_ref):
    cols_ref[...] = jnp.concatenate([rows_ref[...], jnp.zeros((N - 32, L), F32)], axis=0).T
    tile = 128
    lane = iota((tile, W), 1) // HD
    gain = jnp.zeros((1, W), F32)
    for h in range(H):
        gain = jnp.where(iota((1, W), 1) // HD == h, skip_ref[h], gain)
    lower = iota((tile, tile), 0) > iota((tile, tile), 1)
    upper = iota((tile, tile), 0) < iota((tile, tile), 1)
    for i in range(L // tile):
        first, last = i * tile, (i + 1) * tile
        here = slice(first, last)
        scores = dot(query_ref[here, :], key_ref[...])
        cols = cols_ref[here, :]
        since = jnp.exp(cols - cols[0:1])
        until = jnp.exp(cols[tile - 1 : tile] - cols)
        if i > 0:
            edge = rows_ref[0:H, first - 1 : first]
            past = jnp.exp(edge - rows_ref[0:H, 0:first]) * rows_ref[16 : 16 + H, 0:first]
        if last < L:
            edge = rows_ref[H : 2 * H, last - 1 : last]
            coming = jnp.exp(rows_ref[12 : 12 + H, last:L] - edge) * rows_ref[20 : 20 + H, last:L]
        out = jnp.zeros((tile, W), F32)
        for h in range(H):
            gap = jnp.where(
                lower,
                cols[:, 8 + h : 9 + h] - rows_ref[h : h + 1, here],
                rows_ref[12 + h : 13 + h, here] - cols[:, H + h : H + h + 1],
            )
            step = jnp.where(lower, rows_ref[16 + h : 17 + h, here], rows_ref[20 + h : 21 + h, here])
            own = jnp.where(lower | upper, scores[:, here] * jnp.exp(gap) * step, 0.0).astype(BF16)
            pieces = [own]
            if i > 0:
                pieces.insert(0, (scores[:, 0:first] * past[h : h + 1] * since[:, 8 + h : 9 + h]).astype(BF16))
            if last < L:
                pieces.append((scores[:, last:L] * coming[h : h + 1] * until[:, H + h : H + h + 1]).astype(BF16))
            out = jnp.where(lane == h, dot(jnp.concatenate(pieces, axis=1), values_ref[...]), out)
        inner_ref[here, :] = out + gain * values_ref[here, :].astype(F32)


def near_states(got_ref):
    extra = got_ref[:, :, 2 * W : 2 * W + N].reshape(GROUP * SLICE, N)
    decay = jnp.exp(dot(extra, spread(2 * W, 0, 2)))
    order = [NEAR_ORDER.index(j) for j in range(GROUP)]
    states = [got_ref[j, :, 0 : 2 * W].astype(F32) for j in order]
    decays = [decay[SLICE * j : SLICE * (j + 1)] for j in order]
    return states, decays


def totals_kernel(group_ref, got_ref, out_ref):
    g = group_ref[0]
    states, decays = near_states(got_ref)
    forward = states[0][:, :W]
    for j in range(1, GROUP):
        forward = decays[j][:, :W] * forward + states[j][:, :W]
    backward = states[GROUP - 1][:, W:]
    for j in range(GROUP - 2, -1, -1):
        backward = decays[j][:, W:] * backward + states[j][:, W:]
    log = jnp.zeros((SLICE, N), F32)
    for j in range(GROUP):
        log = log + got_ref[j, :, 2 * W : 2 * W + N].astype(F32)
    high = log.astype(BF16).astype(F32)
    log = (high + pltpu.roll(log - high, 16, 1)).astype(BF16)
    forward = forward.astype(BF16)
    backward = backward.astype(BF16)
    for q in range(8):
        out_ref[q, :, 0:W] = jnp.where(FAR_ORDER[q] > g, forward, backward)
        out_ref[q, :, W : W + N] = log


def enter_kernel(group_ref, got_ref, far_ref, out_ref):
    g = group_ref[0]
    states, decays = near_states(got_ref)
    extra = far_ref[:, :, W : W + N].reshape(8 * SLICE, N)
    decay = jnp.exp(dot(extra, spread(2 * W, 0, 4)))
    forward = jnp.zeros((SLICE, W), F32)
    backward = jnp.zeros((SLICE, W), F32)
    for q in range(8):
        slot = FAR_ORDER.index(q)
        rows = slice(SLICE * slot, SLICE * (slot + 1))
        forward = jnp.where(q < g, decay[rows, :W] * forward + far_ref[slot, :, 0:W].astype(F32), forward)
    for q in range(7, -1, -1):
        slot = FAR_ORDER.index(q)
        rows = slice(SLICE * slot, SLICE * (slot + 1))
        backward = jnp.where(q > g, decay[rows, W:] * backward + far_ref[slot, :, 0:W].astype(F32), backward)
    for j in range(GROUP):
        out_ref[NEAR_ORDER.index(j), :, 0:W] = forward.astype(BF16)
        forward = decays[j][:, :W] * forward + states[j][:, :W]
    for j in range(GROUP - 1, -1, -1):
        out_ref[NEAR_ORDER.index(j), :, W : 2 * W] = backward.astype(BF16)
        backward = decays[j][:, W:] * backward + states[j][:, W:]


def mix_kernel(inner_ref, gates_ref, query_ref, enter_ref, rows_ref, hidden_ref):
    cols = jnp.concatenate([rows_ref[24:32], jnp.zeros((N - 8, L), F32)], axis=0).T
    carried = dot(query_ref[...], enter_ref[...]) * widen(cols, 0, 2 * W)
    mix = inner_ref[...] + carried[:, :W] + carried[:, W:]
    gates = gates_ref[...]
    gated = mix * (gates / (1.0 + jnp.exp(-gates)))
    square = gated * gated
    same = (iota((W, W), 0) // HD == iota((W, W), 1) // HD).astype(BF16)
    high = square.astype(BF16)
    low = (square - high.astype(F32)).astype(BF16)
    power = (dot(high, same) + dot(low, same)) * (1.0 / HD)
    hidden_ref[...] = (gated * lax.rsqrt(power + 1e-05)).astype(BF16)


def pair_kernel(core_ref, hidden_ref, w_ref, other_ref, out_ref):
    c = core_ref[0]
    hidden = jnp.concatenate([hidden_ref[c], hidden_ref[1 - c]], axis=1)
    for x in range(XS):
        at = slice(W * x, W * (x + 1))
        out_ref[X_ORDER.index(x)] = dot(hidden, jnp.concatenate([w_ref[:, at], other_ref[:, at]], axis=0)).astype(BF16)


def sum_kernel(pieces_ref, out_ref):
    total = pieces_ref[0].astype(F32) + pieces_ref[1].astype(F32)
    total = total + pieces_ref[2].astype(F32) + pieces_ref[3].astype(F32)
    out_ref[...] = total.astype(BF16)


def call(kernel, name, ins, outs, flops, *operands, touched=1 << 21, scratch=(), out_spec=VMEM, limit=20 << 20):
    return pl.pallas_call(
        kernel,
        name=name,
        in_specs=ins,
        out_specs=[out_spec] * len(outs),
        scratch_shapes=scratch,
        out_shape=[jax.ShapeDtypeStruct(shape, kind) for shape, kind in outs],
        compiler_params=pltpu.CompilerParams(vmem_limit_bytes=limit),
        cost_estimate=pl.CostEstimate(flops=flops, bytes_accessed=touched, transcendentals=1 << 16),
    )(*operands)


def shards(tokens, in_weight, bc_weight, dt_weight, dt_bias, decay_rate, skip_gain, out_weight):
    core = (lax.axis_index("tp").astype(jnp.int32) & 1)[None]
    group = (lax.axis_index("seq").astype(jnp.int32) >> 3)[None]
    (payload,) = call(
        prep_kernel,
        "payload",
        [VMEM, VMEM],
        [((XS, L + W, W), BF16)],
        1,
        tokens,
        bc_weight.T,
        touched=0,
        scratch=[pltpu.VMEM((W, W), BF16), pltpu.SemaphoreType.DMA((2 * XS,))],
        out_spec=HBM,
        limit=(64 << 20) - (64 << 10),
    )
    flat_weight = in_weight.reshape(D, 2 * W)
    steps_weight = dt_weight.transpose(0, 2, 1)
    mine = lax.all_to_all(payload, "tp", 0, 0, axis_index_groups=X_GROUPS, tiled=True)
    own_weight, other_weight = call(
        columns_kernel, "columns", [SMEM, VMEM], [((W, XS * W), BF16)] * 2, 1, core, out_weight
    )
    other_weight = lax.ppermute(other_weight, "tp", SWAP)
    mine, core, group, own_weight, other_weight = lax.optimization_barrier(
        (mine, core, group, own_weight, other_weight)
    )
    theirs = lax.ppermute(mine, "tp", SWAP)
    half, narrow, steps_weight = call(
        half_kernel,
        "half",
        [SMEM, VMEM, VMEM, VMEM],
        [((L, 2 * W), F32), ((80, L), F32), ((SLICE, D), BF16)],
        1 << 30,
        core, mine, flat_weight, steps_weight,
        scratch=[pltpu.VMEM((SLICE, D), F32)],
    )
    values, gates, query, key, rows, message = call(
        project_kernel,
        "project",
        [SMEM, SMEM, SMEM, VMEM, VMEM, VMEM, VMEM, VMEM, VMEM],
        [
            ((L, W), BF16),
            ((L, W), F32),
            ((L, N), BF16),
            ((N, L), BF16),
            ((32, L), F32),
            ((GROUP, SLICE, 2 * W + N), BF16),
        ],
        1 << 31,
        core, dt_bias, decay_rate, mine, theirs, flat_weight, steps_weight, half, narrow,
    )
    near = lax.all_to_all(message, "seq", 0, 0, axis_index_groups=NEAR, tiled=True)
    (inner,) = call(
        inner_kernel,
        "inside",
        [SMEM, VMEM, VMEM, VMEM, VMEM],
        [((L, W), F32)],
        1 << 31,
        skip_gain, query, key, values, rows,
        scratch=[pltpu.VMEM((L, N), F32)],
    )
    (totals,) = call(
        totals_kernel, "totals", [SMEM, VMEM], [((8, SLICE, W + N), BF16)], 1 << 20, group, near
    )
    far = lax.all_to_all(totals, "seq", 0, 0, axis_index_groups=FAR, tiled=True)
    far, inner = lax.optimization_barrier((far, inner))
    (enters,) = call(
        enter_kernel, "enters", [SMEM, VMEM, VMEM], [((GROUP, SLICE, 2 * W), BF16)], 1 << 20, group, near, far
    )
    enter = lax.all_to_all(enters, "seq", 0, 0, axis_index_groups=NEAR, tiled=True).reshape(N, 2 * W)
    (hidden,) = call(
        mix_kernel, "mix", [VMEM] * 5, [((L, W), BF16)], 1 << 28, inner, gates, query, enter, rows
    )
    hidden = lax.all_gather(hidden, "tp", axis_index_groups=PAIRS)
    (paired,) = call(
        pair_kernel, "pair", [SMEM, VMEM, VMEM, VMEM], [((XS, L, W), BF16)], 1 << 29, core, hidden, own_weight, other_weight,
        touched=1 << 25,
    )
    pieces = lax.all_to_all(paired, "tp", 0, 0, axis_index_groups=X_GROUPS, tiled=True)
    return call(sum_kernel, "sum", [VMEM], [((L, W), BF16)], 1 << 20, pieces)[0]


def solution(mesh):
    in_specs = (
        P("seq", "tp"),
        P(None, None, "tp"),
        P(None, "tp"),
        P(None, None, "tp"),
        P(None, "tp"),
        P("tp"),
        P("tp"),
        P("tp", None),
    )
    out_specs = P("seq", "tp")
    return jax.shard_map(shards, mesh=mesh, in_specs=in_specs, out_specs=out_specs, check_vma=False)
```

```python
import jax
import jax.numpy as jnp
from jax import lax
from jax.experimental import pallas as pl
from jax.experimental.pallas import tpu as pltpu
from jax.sharding import PartitionSpec as P

F32 = jnp.float32
BF16 = jnp.bfloat16
L = 512
D = 2048
W = 256
H = 4
HD = 64
N = 128
XS = 4
GROUP = 8
SLICE = N // GROUP

X_ORDER = [2, 3, 1, 0]
X_GROUPS = [[2 * x + c for x in X_ORDER] for c in range(2)]
SUM_ORDER = [2, 3, 1, 0]
SUM_GROUPS = [[2 * x + c for x in SUM_ORDER] for c in range(2)]
PAIRS = [[2 * x, 2 * x + 1] for x in range(XS)]
SWAP = [(i, i ^ 1) for i in range(8)]
NEAR_ORDER = [6, 7, 5, 4, 3, 2, 1, 0]
NEAR = [[GROUP * g + j for j in NEAR_ORDER] for g in range(8)]
FAR_ORDER = [5, 4, 6, 7, 3, 2, 1, 0]
FAR = [[GROUP * g + j for g in FAR_ORDER] for j in range(GROUP)]

VMEM = pl.BlockSpec(memory_space=pltpu.VMEM)
SMEM = pl.BlockSpec(memory_space=pltpu.SMEM)
HBM = pl.BlockSpec(memory_space=pltpu.HBM)
NN = (((1,), (0,)), ((), ()))
NT = (((1,), (1,)), ((), ()))


def dot(a, b, dims=NN):
    return lax.dot_general(a, b, dims, preferred_element_type=F32)


def iota(shape, axis):
    return lax.broadcasted_iota(jnp.int32, shape, axis)


def spread(width, base, copies):
    row = iota((N, width), 0)
    want = iota((N, width), 1) // HD + base
    hit = row == want
    for q in range(1, copies):
        hit = hit | (row == want + 8 * q)
    return hit.astype(BF16)


def widen(cols, base, width):
    pick = spread(width, base, 1)
    high = cols.astype(BF16)
    low = (cols - high.astype(F32)).astype(BF16)
    return dot(high, pick) + dot(low, pick)


def column(ref, rows):
    index = iota((2 * H, 1), 0)
    out = jnp.zeros((2 * H, 1), F32)
    for i in range(2 * H):
        out = jnp.where(index == i, rows(ref, i), out)
    return out


def prep_kernel(tokens_ref, bc_ref, out_ref, rows_ref, sems):
    copies = []
    for x in range(XS):
        copies.append(pltpu.make_async_copy(tokens_ref, out_ref.at[x, pl.ds(0, L)], sems.at[x]))
        copies[-1].start()
    for b in range(8):
        rows_ref[32 * b : 32 * (b + 1), :] = bc_ref[:, W * b : W * (b + 1)]
    for x in range(XS):
        copies.append(pltpu.make_async_copy(rows_ref, out_ref.at[x, pl.ds(L, W)], sems.at[XS + x]))
        copies[-1].start()
    for copy in copies:
        copy.wait()


def columns_kernel(core_ref, w_ref, own_ref, out_ref):
    for x in range(XS):
        for ref, c in ((own_ref, core_ref[0]), (out_ref, 1 - core_ref[0])):
            ref[:, W * x : W * (x + 1)] = w_ref[:, pl.ds(pl.multiple_of((2 * x + c) * W, W), W)]


def bc_columns(ref, first, j):
    row = pl.multiple_of(L + j * 32, 32)
    return [ref[X_ORDER.index(x), pl.ds(row, 32), :] for x in (first, first + 1)]


def wide_part(ref, w_ref, c):
    total = None
    for x in range(XS):
        rows = pl.ds(pl.multiple_of((2 * x + c) * W, W), W)
        term = dot(ref[X_ORDER.index(x), 0:L, :], w_ref[rows, :])
        total = term if total is None else total + term
    return total


def narrow_part(ref, refs, d_ref, c):
    total = None
    for x in range(XS):
        j = 2 * x + c
        pieces = [piece for r in refs for piece in bc_columns(r, 0, j)]
        if d_ref is not None:
            pieces.append(d_ref[:, pl.ds(pl.multiple_of(j * W, W), W)])
        term = dot(jnp.concatenate(pieces, axis=0), ref[X_ORDER.index(x), 0:L, :], NT)
        total = term if total is None else total + term
    return total


def query_part(ref, refs, c):
    total = None
    for x in range(XS):
        pieces = [piece for r in refs for piece in bc_columns(r, 2, 2 * x + c)]
        term = dot(ref[X_ORDER.index(x), 0:L, :], jnp.concatenate(pieces, axis=0), NT)
        total = term if total is None else total + term
    return total


def half_kernel(core_ref, a_ref, w_ref, d_ref, wide_ref, narrow_ref, steps_ref, high_ref):
    c = core_ref[0]
    high_ref[...] = jnp.zeros((SLICE, D), F32)
    for i in range(2):
        high_ref[H * i : H * (i + 1), :] = d_ref[i].astype(F32)
    steps_ref[...] = high_ref[...].astype(BF16)
    wide_ref[...] = wide_part(a_ref, w_ref, c)
    narrow_ref[...] = narrow_part(a_ref, (a_ref,), steps_ref, c)


def project_kernel(
    core_ref, bias_ref, rate_ref, a_ref, b_ref, w_ref, d_ref, half_ref, narrow_ref,
    values_ref, gates_ref, query_ref, key_ref, rows_ref, message_ref,
):
    c = core_ref[0]
    later = narrow_part(b_ref, (a_ref, b_ref), d_ref, 1 - c)
    earlier = narrow_ref[...]
    key = jnp.concatenate(
        [earlier[0:64] + later[0:64], narrow_part(a_ref, (b_ref,), None, c) + later[64:128]], axis=0
    ).astype(BF16)
    key_ref[...] = key
    both = half_ref[...] + wide_part(b_ref, w_ref, 1 - c)
    values = both[:, :W].astype(BF16)
    values_ref[...] = values
    gates_ref[...] = both[:, W:]
    query_ref[...] = (query_part(a_ref, (a_ref, b_ref), c) + query_part(b_ref, (a_ref, b_ref), 1 - c)).astype(BF16)
    raw = (earlier[64:72] + later[128:136]) + column(bias_ref, lambda r, i: r[i // H, i % H])
    steps = jnp.maximum(raw, 0.0) + jnp.log1p(jnp.exp(-jnp.abs(raw)))
    logs = -column(rate_ref, lambda r, i: r[i % H]) * steps
    p1 = logs.astype(BF16)
    rest = logs - p1.astype(F32)
    p2 = rest.astype(BF16)
    p3 = (rest - p2.astype(F32)).astype(BF16)
    running = (iota((L, L), 0) <= iota((L, L), 1)).astype(BF16)
    parts = jnp.concatenate([p1.astype(F32), p2.astype(F32), p3.astype(F32), jnp.zeros((8, L), F32)], axis=0)
    summed = dot(parts.astype(BF16), running)
    upto = summed[0:8] + summed[8:16] + summed[16:24]
    before = upto - logs
    total = upto[:, L - 1 : L]
    forward = iota((2 * H, L), 0) < H
    scale = jnp.exp(jnp.where(forward, total - upto, before)) * steps
    reach = jnp.exp(jnp.where(forward, before, total - upto))
    rows_ref[...] = jnp.concatenate([upto, before, steps, reach], axis=0)

    wide = key.astype(F32)
    scaled = jnp.concatenate([(wide * scale[i : i + 1]).astype(BF16) for i in range(2 * H)], axis=0)
    state = dot(scaled, values)
    head = iota((N, W), 1) // HD
    sides = []
    for first in (0, H):
        out = state[N * first : N * (first + 1)]
        for h in range(1, H):
            out = jnp.where(head == h, state[N * (first + h) : N * (first + h + 1)], out)
        sides.append(out.astype(BF16))
    lane = iota((2 * H, N), 1)
    mine_only = (iota((2 * H, N), 0) == lane % 8) & (lane < 16)
    last = jnp.sum(jnp.where(mine_only, total, 0.0), axis=0, keepdims=True)
    high = last.astype(BF16).astype(F32)
    extra = jnp.where(iota((1, N), 1) < 8, high, last - high)
    extra = jnp.broadcast_to(extra, (SLICE, N)).astype(BF16)
    for k in range(GROUP):
        for i in range(2):
            message_ref[k, :, W * i : W * (i + 1)] = sides[i][SLICE * k : SLICE * (k + 1)]
        message_ref[k, :, 2 * W : 2 * W + N] = extra


def inner_kernel(skip_ref, query_ref, key_ref, values_ref, rows_ref, inner_ref, cols_ref):
    cols_ref[...] = jnp.concatenate([rows_ref[...], jnp.zeros((N - 32, L), F32)], axis=0).T
    tile = 128
    lane = iota((tile, W), 1) // HD
    gain = jnp.zeros((1, W), F32)
    for h in range(H):
        gain = jnp.where(iota((1, W), 1) // HD == h, skip_ref[h], gain)
    lower = iota((tile, tile), 0) > iota((tile, tile), 1)
    upper = iota((tile, tile), 0) < iota((tile, tile), 1)
    for i in range(L // tile):
        first, last = i * tile, (i + 1) * tile
        here = slice(first, last)
        scores = dot(query_ref[here, :], key_ref[...])
        cols = cols_ref[here, :]
        since = jnp.exp(cols - cols[0:1])
        until = jnp.exp(cols[tile - 1 : tile] - cols)
        if i > 0:
            edge = rows_ref[0:H, first - 1 : first]
            past = jnp.exp(edge - rows_ref[0:H, 0:first]) * rows_ref[16 : 16 + H, 0:first]
        if last < L:
            edge = rows_ref[H : 2 * H, last - 1 : last]
            coming = jnp.exp(rows_ref[12 : 12 + H, last:L] - edge) * rows_ref[20 : 20 + H, last:L]
        out = jnp.zeros((tile, W), F32)
        for h in range(H):
            gap = jnp.where(
                lower,
                cols[:, 8 + h : 9 + h] - rows_ref[h : h + 1, here],
                rows_ref[12 + h : 13 + h, here] - cols[:, H + h : H + h + 1],
            )
            step = jnp.where(lower, rows_ref[16 + h : 17 + h, here], rows_ref[20 + h : 21 + h, here])
            own = jnp.where(lower | upper, scores[:, here] * jnp.exp(gap) * step, 0.0).astype(BF16)
            pieces = [own]
            if i > 0:
                pieces.insert(0, (scores[:, 0:first] * past[h : h + 1] * since[:, 8 + h : 9 + h]).astype(BF16))
            if last < L:
                pieces.append((scores[:, last:L] * coming[h : h + 1] * until[:, H + h : H + h + 1]).astype(BF16))
            out = jnp.where(lane == h, dot(jnp.concatenate(pieces, axis=1), values_ref[...]), out)
        inner_ref[here, :] = out + gain * values_ref[here, :].astype(F32)


def near_states(got_ref):
    extra = got_ref[:, :, 2 * W : 2 * W + N].reshape(GROUP * SLICE, N)
    decay = jnp.exp(dot(extra, spread(2 * W, 0, 2)))
    order = [NEAR_ORDER.index(j) for j in range(GROUP)]
    states = [got_ref[j, :, 0 : 2 * W].astype(F32) for j in order]
    decays = [decay[SLICE * j : SLICE * (j + 1)] for j in order]
    return states, decays


def totals_kernel(group_ref, got_ref, out_ref):
    g = group_ref[0]
    states, decays = near_states(got_ref)
    forward = states[0][:, :W]
    for j in range(1, GROUP):
        forward = decays[j][:, :W] * forward + states[j][:, :W]
    backward = states[GROUP - 1][:, W:]
    for j in range(GROUP - 2, -1, -1):
        backward = decays[j][:, W:] * backward + states[j][:, W:]
    log = jnp.zeros((SLICE, N), F32)
    for j in range(GROUP):
        log = log + got_ref[j, :, 2 * W : 2 * W + N].astype(F32)
    high = log.astype(BF16).astype(F32)
    log = (high + pltpu.roll(log - high, 16, 1)).astype(BF16)
    forward = forward.astype(BF16)
    backward = backward.astype(BF16)
    for q in range(8):
        out_ref[q, :, 0:W] = jnp.where(FAR_ORDER[q] > g, forward, backward)
        out_ref[q, :, W : W + N] = log


def enter_kernel(group_ref, got_ref, far_ref, out_ref):
    g = group_ref[0]
    states, decays = near_states(got_ref)
    extra = far_ref[:, :, W : W + N].reshape(8 * SLICE, N)
    decay = jnp.exp(dot(extra, spread(2 * W, 0, 4)))
    forward = jnp.zeros((SLICE, W), F32)
    backward = jnp.zeros((SLICE, W), F32)
    for q in range(8):
        slot = FAR_ORDER.index(q)
        rows = slice(SLICE * slot, SLICE * (slot + 1))
        forward = jnp.where(q < g, decay[rows, :W] * forward + far_ref[slot, :, 0:W].astype(F32), forward)
    for q in range(7, -1, -1):
        slot = FAR_ORDER.index(q)
        rows = slice(SLICE * slot, SLICE * (slot + 1))
        backward = jnp.where(q > g, decay[rows, W:] * backward + far_ref[slot, :, 0:W].astype(F32), backward)
    for j in range(GROUP):
        out_ref[NEAR_ORDER.index(j), :, 0:W] = forward.astype(BF16)
        forward = decays[j][:, :W] * forward + states[j][:, :W]
    for j in range(GROUP - 1, -1, -1):
        out_ref[NEAR_ORDER.index(j), :, W : 2 * W] = backward.astype(BF16)
        backward = decays[j][:, W:] * backward + states[j][:, W:]


def mix_kernel(inner_ref, gates_ref, query_ref, enter_ref, rows_ref, hidden_ref):
    cols = jnp.concatenate([rows_ref[24:32], jnp.zeros((N - 8, L), F32)], axis=0).T
    carried = dot(query_ref[...], enter_ref[...]) * widen(cols, 0, 2 * W)
    mix = inner_ref[...] + carried[:, :W] + carried[:, W:]
    gates = gates_ref[...]
    gated = mix * (gates / (1.0 + jnp.exp(-gates)))
    square = gated * gated
    same = (iota((W, W), 0) // HD == iota((W, W), 1) // HD).astype(BF16)
    high = square.astype(BF16)
    low = (square - high.astype(F32)).astype(BF16)
    power = (dot(high, same) + dot(low, same)) * (1.0 / HD)
    hidden_ref[...] = (gated * lax.rsqrt(power + 1e-05)).astype(BF16)


def pair_kernel(core_ref, hidden_ref, w_ref, other_ref, out_ref):
    c = core_ref[0]
    hidden = jnp.concatenate([hidden_ref[c], hidden_ref[1 - c]], axis=1)
    for x in range(XS):
        at = slice(W * x, W * (x + 1))
        out_ref[SUM_ORDER.index(x)] = dot(hidden, jnp.concatenate([w_ref[:, at], other_ref[:, at]], axis=0)).astype(BF16)


def sum_kernel(pieces_ref, out_ref):
    total = pieces_ref[0].astype(F32) + pieces_ref[1].astype(F32)
    total = total + pieces_ref[2].astype(F32) + pieces_ref[3].astype(F32)
    out_ref[...] = total.astype(BF16)


def call(kernel, name, ins, outs, flops, *operands, touched=1 << 21, scratch=(), out_spec=VMEM, limit=20 << 20):
    return pl.pallas_call(
        kernel,
        name=name,
        in_specs=ins,
        out_specs=[out_spec] * len(outs),
        scratch_shapes=scratch,
        out_shape=[jax.ShapeDtypeStruct(shape, kind) for shape, kind in outs],
        compiler_params=pltpu.CompilerParams(vmem_limit_bytes=limit),
        cost_estimate=pl.CostEstimate(flops=flops, bytes_accessed=touched, transcendentals=1 << 16),
    )(*operands)


def shards(tokens, in_weight, bc_weight, dt_weight, dt_bias, decay_rate, skip_gain, out_weight):
    core = (lax.axis_index("tp").astype(jnp.int32) & 1)[None]
    group = (lax.axis_index("seq").astype(jnp.int32) >> 3)[None]
    (payload,) = call(
        prep_kernel,
        "payload",
        [VMEM, VMEM],
        [((XS, L + W, W), BF16)],
        1,
        tokens,
        bc_weight.T,
        touched=0,
        scratch=[pltpu.VMEM((W, W), BF16), pltpu.SemaphoreType.DMA((2 * XS,))],
        out_spec=HBM,
        limit=(64 << 20) - (64 << 10),
    )
    flat_weight = in_weight.reshape(D, 2 * W)
    steps_weight = dt_weight.transpose(0, 2, 1)
    mine = lax.all_to_all(payload, "tp", 0, 0, axis_index_groups=X_GROUPS, tiled=True)
    own_weight, other_weight = call(
        columns_kernel, "columns", [SMEM, VMEM], [((W, XS * W), BF16)] * 2, 1, core, out_weight
    )
    other_weight = lax.ppermute(other_weight, "tp", SWAP)
    mine, core, group, own_weight, other_weight = lax.optimization_barrier(
        (mine, core, group, own_weight, other_weight)
    )
    theirs = lax.ppermute(mine, "tp", SWAP)
    half, narrow, steps_weight = call(
        half_kernel,
        "half",
        [SMEM, VMEM, VMEM, VMEM],
        [((L, 2 * W), F32), ((80, L), F32), ((SLICE, D), BF16)],
        1 << 30,
        core, mine, flat_weight, steps_weight,
        scratch=[pltpu.VMEM((SLICE, D), F32)],
    )
    values, gates, query, key, rows, message = call(
        project_kernel,
        "project",
        [SMEM, SMEM, SMEM, VMEM, VMEM, VMEM, VMEM, VMEM, VMEM],
        [
            ((L, W), BF16),
            ((L, W), F32),
            ((L, N), BF16),
            ((N, L), BF16),
            ((32, L), F32),
            ((GROUP, SLICE, 2 * W + N), BF16),
        ],
        1 << 31,
        core, dt_bias, decay_rate, mine, theirs, flat_weight, steps_weight, half, narrow,
    )
    near = lax.all_to_all(message, "seq", 0, 0, axis_index_groups=NEAR, tiled=True)
    (inner,) = call(
        inner_kernel,
        "inside",
        [SMEM, VMEM, VMEM, VMEM, VMEM],
        [((L, W), F32)],
        1 << 31,
        skip_gain, query, key, values, rows,
        scratch=[pltpu.VMEM((L, N), F32)],
    )
    (totals,) = call(
        totals_kernel, "totals", [SMEM, VMEM], [((8, SLICE, W + N), BF16)], 1 << 20, group, near
    )
    far = lax.all_to_all(totals, "seq", 0, 0, axis_index_groups=FAR, tiled=True)
    far, inner = lax.optimization_barrier((far, inner))
    (enters,) = call(
        enter_kernel, "enters", [SMEM, VMEM, VMEM], [((GROUP, SLICE, 2 * W), BF16)], 1 << 20, group, near, far
    )
    enter = lax.all_to_all(enters, "seq", 0, 0, axis_index_groups=NEAR, tiled=True).reshape(N, 2 * W)
    (hidden,) = call(
        mix_kernel, "mix", [VMEM] * 5, [((L, W), BF16)], 1 << 28, inner, gates, query, enter, rows
    )
    hidden = lax.all_gather(hidden, "tp", axis_index_groups=PAIRS)
    (paired,) = call(
        pair_kernel, "pair", [SMEM, VMEM, VMEM, VMEM], [((XS, L, W), BF16)], 1 << 29, core, hidden, own_weight, other_weight,
        touched=1 << 25,
    )
    pieces = lax.all_to_all(paired, "tp", 0, 0, axis_index_groups=SUM_GROUPS, tiled=True)
    return call(sum_kernel, "sum", [VMEM], [((L, W), BF16)], 1 << 20, pieces)[0]


def solution(mesh):
    in_specs = (
        P("seq", "tp"),
        P(None, None, "tp"),
        P(None, "tp"),
        P(None, None, "tp"),
        P(None, "tp"),
        P("tp"),
        P("tp"),
        P("tp", None),
    )
    out_specs = P("seq", "tp")
    return jax.shard_map(shards, mesh=mesh, in_specs=in_specs, out_specs=out_specs, check_vma=False)
```

```python
import jax
import jax.numpy as jnp
from jax import lax
from jax.experimental import pallas as pl
from jax.experimental.pallas import tpu as pltpu
from jax.sharding import PartitionSpec as P

F32 = jnp.float32
BF16 = jnp.bfloat16
L = 512
D = 2048
W = 256
H = 4
HD = 64
N = 128
XS = 4
GROUP = 8
SLICE = N // GROUP

X_ORDER = [2, 3, 1, 0]
X_GROUPS = [[2 * x + c for x in X_ORDER] for c in range(2)]
SUM_ORDER = [2, 3, 1, 0]
SUM_GROUPS = [[2 * x + c for x in SUM_ORDER] for c in range(2)]
PAIRS = [[2 * x, 2 * x + 1] for x in range(XS)]
SWAP = [(i, i ^ 1) for i in range(8)]
NEAR_ORDER = [6, 7, 5, 4, 3, 2, 1, 0]
NEAR = [[GROUP * g + j for j in NEAR_ORDER] for g in range(8)]
FAR_ORDER = [5, 4, 6, 7, 3, 2, 1, 0]
FAR = [[GROUP * g + j for g in FAR_ORDER] for j in range(GROUP)]

VMEM = pl.BlockSpec(memory_space=pltpu.VMEM)
SMEM = pl.BlockSpec(memory_space=pltpu.SMEM)
HBM = pl.BlockSpec(memory_space=pltpu.HBM)
NN = (((1,), (0,)), ((), ()))
NT = (((1,), (1,)), ((), ()))


def dot(a, b, dims=NN):
    return lax.dot_general(a, b, dims, preferred_element_type=F32)


def iota(shape, axis):
    return lax.broadcasted_iota(jnp.int32, shape, axis)


def spread(width, base, copies):
    row = iota((N, width), 0)
    want = iota((N, width), 1) // HD + base
    hit = row == want
    for q in range(1, copies):
        hit = hit | (row == want + 8 * q)
    return hit.astype(BF16)


def widen(cols, base, width):
    pick = spread(width, base, 1)
    high = cols.astype(BF16)
    low = (cols - high.astype(F32)).astype(BF16)
    return dot(high, pick) + dot(low, pick)


def column(ref, rows):
    index = iota((2 * H, 1), 0)
    out = jnp.zeros((2 * H, 1), F32)
    for i in range(2 * H):
        out = jnp.where(index == i, rows(ref, i), out)
    return out


def prep_kernel(tokens_ref, bc_ref, out_ref, rows_ref, sems):
    copies = []
    for x in range(XS):
        copies.append(pltpu.make_async_copy(tokens_ref, out_ref.at[x, pl.ds(0, L)], sems.at[x]))
        copies[-1].start()
    for b in range(8):
        rows_ref[32 * b : 32 * (b + 1), :] = bc_ref[:, W * b : W * (b + 1)]
    for x in range(XS):
        copies.append(pltpu.make_async_copy(rows_ref, out_ref.at[x, pl.ds(L, W)], sems.at[XS + x]))
        copies[-1].start()
    for copy in copies:
        copy.wait()


def columns_kernel(core_ref, w_ref, own_ref, out_ref):
    for x in range(XS):
        for ref, c in ((own_ref, core_ref[0]), (out_ref, 1 - core_ref[0])):
            ref[:, W * x : W * (x + 1)] = w_ref[:, pl.ds(pl.multiple_of((2 * x + c) * W, W), W)]


def bc_columns(ref, first, j):
    row = pl.multiple_of(L + j * 32, 32)
    return [ref[X_ORDER.index(x), pl.ds(row, 32), :] for x in (first, first + 1)]


def wide_part(ref, w_ref, c):
    total = None
    for x in range(XS):
        rows = pl.ds(pl.multiple_of((2 * x + c) * W, W), W)
        term = dot(ref[X_ORDER.index(x), 0:L, :], w_ref[rows, :])
        total = term if total is None else total + term
    return total


def narrow_part(ref, refs, d_ref, c):
    total = None
    for x in range(XS):
        j = 2 * x + c
        pieces = [piece for first in (0, 2) for r in refs for piece in bc_columns(r, first, j)]
        if d_ref is not None:
            pieces.append(d_ref[:, pl.ds(pl.multiple_of(j * W, W), W)])
        term = dot(jnp.concatenate(pieces, axis=0), ref[X_ORDER.index(x), 0:L, :], NT)
        total = term if total is None else total + term
    return total


def half_kernel(core_ref, a_ref, w_ref, d_ref, wide_ref, narrow_ref, steps_ref, high_ref):
    c = core_ref[0]
    high_ref[...] = jnp.zeros((SLICE, D), F32)
    for i in range(2):
        high_ref[H * i : H * (i + 1), :] = d_ref[i].astype(F32)
    steps_ref[...] = high_ref[...].astype(BF16)
    wide_ref[...] = wide_part(a_ref, w_ref, c)
    narrow_ref[...] = narrow_part(a_ref, (a_ref,), steps_ref, c)


def project_kernel(
    core_ref, bias_ref, rate_ref, a_ref, b_ref, w_ref, d_ref, half_ref, narrow_ref,
    values_ref, gates_ref, query_ref, key_ref, rows_ref, message_ref,
):
    c = core_ref[0]
    later = narrow_part(b_ref, (a_ref, b_ref), d_ref, 1 - c)
    earlier = narrow_ref[...]
    crossed = narrow_part(a_ref, (b_ref,), None, c)
    key = jnp.concatenate([earlier[0:64] + later[0:64], crossed[0:64] + later[64:128]], axis=0).astype(BF16)
    key_ref[...] = key
    query = jnp.concatenate([earlier[64:128] + later[128:192], crossed[64:128] + later[192:256]], axis=0)
    query_ref[...] = query.T.astype(BF16)
    both = half_ref[...] + wide_part(b_ref, w_ref, 1 - c)
    gates_ref[...] = both[:, W:]
    values = both[:, :W].astype(BF16)
    values_ref[...] = values
    raw = (earlier[128:136] + later[256:264]) + column(bias_ref, lambda r, i: r[i // H, i % H])
    steps = jnp.maximum(raw, 0.0) + jnp.log1p(jnp.exp(-jnp.abs(raw)))
    logs = -column(rate_ref, lambda r, i: r[i % H]) * steps
    p1 = logs.astype(BF16)
    rest = logs - p1.astype(F32)
    p2 = rest.astype(BF16)
    p3 = (rest - p2.astype(F32)).astype(BF16)
    running = (iota((L, L), 0) <= iota((L, L), 1)).astype(BF16)
    parts = jnp.concatenate([p1.astype(F32), p2.astype(F32), p3.astype(F32), jnp.zeros((8, L), F32)], axis=0)
    summed = dot(parts.astype(BF16), running)
    upto = summed[0:8] + summed[8:16] + summed[16:24]
    before = upto - logs
    total = upto[:, L - 1 : L]
    forward = iota((2 * H, L), 0) < H
    scale = jnp.exp(jnp.where(forward, total - upto, before)) * steps
    reach = jnp.exp(jnp.where(forward, before, total - upto))
    rows_ref[...] = jnp.concatenate([upto, before, steps, reach], axis=0)

    wide = key.astype(F32)
    scaled = jnp.concatenate([(wide * scale[i : i + 1]).astype(BF16) for i in range(2 * H)], axis=0)
    state = dot(scaled, values)
    head = iota((N, W), 1) // HD
    sides = []
    for first in (0, H):
        out = state[N * first : N * (first + 1)]
        for h in range(1, H):
            out = jnp.where(head == h, state[N * (first + h) : N * (first + h + 1)], out)
        sides.append(out.astype(BF16))
    lane = iota((2 * H, N), 1)
    mine_only = (iota((2 * H, N), 0) == lane % 8) & (lane < 16)
    last = jnp.sum(jnp.where(mine_only, total, 0.0), axis=0, keepdims=True)
    high = last.astype(BF16).astype(F32)
    extra = jnp.where(iota((1, N), 1) < 8, high, last - high)
    extra = jnp.broadcast_to(extra, (SLICE, N)).astype(BF16)
    for k in range(GROUP):
        for i in range(2):
            message_ref[k, :, W * i : W * (i + 1)] = sides[i][SLICE * k : SLICE * (k + 1)]
        message_ref[k, :, 2 * W : 2 * W + N] = extra


def inner_kernel(skip_ref, query_ref, key_ref, values_ref, rows_ref, inner_ref, cols_ref):
    cols_ref[...] = jnp.concatenate([rows_ref[...], jnp.zeros((N - 32, L), F32)], axis=0).T
    tile = 128
    lane = iota((tile, W), 1) // HD
    gain = jnp.zeros((1, W), F32)
    for h in range(H):
        gain = jnp.where(iota((1, W), 1) // HD == h, skip_ref[h], gain)
    lower = iota((tile, tile), 0) > iota((tile, tile), 1)
    upper = iota((tile, tile), 0) < iota((tile, tile), 1)
    for i in range(L // tile):
        first, last = i * tile, (i + 1) * tile
        here = slice(first, last)
        scores = dot(query_ref[here, :], key_ref[...])
        cols = cols_ref[here, :]
        since = jnp.exp(cols - cols[0:1])
        until = jnp.exp(cols[tile - 1 : tile] - cols)
        if i > 0:
            edge = rows_ref[0:H, first - 1 : first]
            past = jnp.exp(edge - rows_ref[0:H, 0:first]) * rows_ref[16 : 16 + H, 0:first]
        if last < L:
            edge = rows_ref[H : 2 * H, last - 1 : last]
            coming = jnp.exp(rows_ref[12 : 12 + H, last:L] - edge) * rows_ref[20 : 20 + H, last:L]
        out = jnp.zeros((tile, W), F32)
        for h in range(H):
            gap = jnp.where(
                lower,
                cols[:, 8 + h : 9 + h] - rows_ref[h : h + 1, here],
                rows_ref[12 + h : 13 + h, here] - cols[:, H + h : H + h + 1],
            )
            step = jnp.where(lower, rows_ref[16 + h : 17 + h, here], rows_ref[20 + h : 21 + h, here])
            own = jnp.where(lower | upper, scores[:, here] * jnp.exp(gap) * step, 0.0).astype(BF16)
            pieces = [own]
            if i > 0:
                pieces.insert(0, (scores[:, 0:first] * past[h : h + 1] * since[:, 8 + h : 9 + h]).astype(BF16))
            if last < L:
                pieces.append((scores[:, last:L] * coming[h : h + 1] * until[:, H + h : H + h + 1]).astype(BF16))
            out = jnp.where(lane == h, dot(jnp.concatenate(pieces, axis=1), values_ref[...]), out)
        inner_ref[here, :] = out + gain * values_ref[here, :].astype(F32)


def near_states(got_ref):
    extra = got_ref[:, :, 2 * W : 2 * W + N].reshape(GROUP * SLICE, N)
    decay = jnp.exp(dot(extra, spread(2 * W, 0, 2)))
    order = [NEAR_ORDER.index(j) for j in range(GROUP)]
    states = [got_ref[j, :, 0 : 2 * W].astype(F32) for j in order]
    decays = [decay[SLICE * j : SLICE * (j + 1)] for j in order]
    return states, decays


def totals_kernel(group_ref, got_ref, out_ref):
    g = group_ref[0]
    states, decays = near_states(got_ref)
    forward = states[0][:, :W]
    for j in range(1, GROUP):
        forward = decays[j][:, :W] * forward + states[j][:, :W]
    backward = states[GROUP - 1][:, W:]
    for j in range(GROUP - 2, -1, -1):
        backward = decays[j][:, W:] * backward + states[j][:, W:]
    log = jnp.zeros((SLICE, N), F32)
    for j in range(GROUP):
        log = log + got_ref[j, :, 2 * W : 2 * W + N].astype(F32)
    high = log.astype(BF16).astype(F32)
    log = (high + pltpu.roll(log - high, 16, 1)).astype(BF16)
    forward = forward.astype(BF16)
    backward = backward.astype(BF16)
    for q in range(8):
        out_ref[q, :, 0:W] = jnp.where(FAR_ORDER[q] > g, forward, backward)
        out_ref[q, :, W : W + N] = log


def enter_kernel(group_ref, got_ref, far_ref, out_ref):
    g = group_ref[0]
    states, decays = near_states(got_ref)
    extra = far_ref[:, :, W : W + N].reshape(8 * SLICE, N)
    decay = jnp.exp(dot(extra, spread(2 * W, 0, 4)))
    forward = jnp.zeros((SLICE, W), F32)
    backward = jnp.zeros((SLICE, W), F32)
    for q in range(8):
        slot = FAR_ORDER.index(q)
        rows = slice(SLICE * slot, SLICE * (slot + 1))
        forward = jnp.where(q < g, decay[rows, :W] * forward + far_ref[slot, :, 0:W].astype(F32), forward)
    for q in range(7, -1, -1):
        slot = FAR_ORDER.index(q)
        rows = slice(SLICE * slot, SLICE * (slot + 1))
        backward = jnp.where(q > g, decay[rows, W:] * backward + far_ref[slot, :, 0:W].astype(F32), backward)
    for j in range(GROUP):
        out_ref[NEAR_ORDER.index(j), :, 0:W] = forward.astype(BF16)
        forward = decays[j][:, :W] * forward + states[j][:, :W]
    for j in range(GROUP - 1, -1, -1):
        out_ref[NEAR_ORDER.index(j), :, W : 2 * W] = backward.astype(BF16)
        backward = decays[j][:, W:] * backward + states[j][:, W:]


def mix_kernel(inner_ref, gates_ref, query_ref, enter_ref, rows_ref, hidden_ref):
    cols = jnp.concatenate([rows_ref[24:32], jnp.zeros((N - 8, L), F32)], axis=0).T
    carried = dot(query_ref[...], enter_ref[...]) * widen(cols, 0, 2 * W)
    mix = inner_ref[...] + carried[:, :W] + carried[:, W:]
    gates = gates_ref[...]
    gated = mix * (gates / (1.0 + jnp.exp(-gates)))
    square = gated * gated
    same = (iota((W, W), 0) // HD == iota((W, W), 1) // HD).astype(BF16)
    high = square.astype(BF16)
    low = (square - high.astype(F32)).astype(BF16)
    power = (dot(high, same) + dot(low, same)) * (1.0 / HD)
    hidden_ref[...] = (gated * lax.rsqrt(power + 1e-05)).astype(BF16)


def pair_kernel(core_ref, hidden_ref, w_ref, other_ref, out_ref):
    c = core_ref[0]
    hidden = jnp.concatenate([hidden_ref[c], hidden_ref[1 - c]], axis=1)
    for x in range(XS):
        at = slice(W * x, W * (x + 1))
        out_ref[SUM_ORDER.index(x)] = dot(hidden, jnp.concatenate([w_ref[:, at], other_ref[:, at]], axis=0)).astype(BF16)


def sum_kernel(pieces_ref, out_ref):
    total = pieces_ref[0].astype(F32) + pieces_ref[1].astype(F32)
    total = total + pieces_ref[2].astype(F32) + pieces_ref[3].astype(F32)
    out_ref[...] = total.astype(BF16)


def call(kernel, name, ins, outs, flops, *operands, touched=1 << 21, scratch=(), out_spec=VMEM, limit=20 << 20):
    return pl.pallas_call(
        kernel,
        name=name,
        in_specs=ins,
        out_specs=[out_spec] * len(outs),
        scratch_shapes=scratch,
        out_shape=[jax.ShapeDtypeStruct(shape, kind) for shape, kind in outs],
        compiler_params=pltpu.CompilerParams(vmem_limit_bytes=limit),
        cost_estimate=pl.CostEstimate(flops=flops, bytes_accessed=touched, transcendentals=1 << 16),
    )(*operands)


def shards(tokens, in_weight, bc_weight, dt_weight, dt_bias, decay_rate, skip_gain, out_weight):
    core = (lax.axis_index("tp").astype(jnp.int32) & 1)[None]
    group = (lax.axis_index("seq").astype(jnp.int32) >> 3)[None]
    (payload,) = call(
        prep_kernel,
        "payload",
        [VMEM, VMEM],
        [((XS, L + W, W), BF16)],
        1,
        tokens,
        bc_weight.T,
        touched=0,
        scratch=[pltpu.VMEM((W, W), BF16), pltpu.SemaphoreType.DMA((2 * XS,))],
        out_spec=HBM,
        limit=(64 << 20) - (64 << 10),
    )
    flat_weight = in_weight.reshape(D, 2 * W)
    steps_weight = dt_weight.transpose(0, 2, 1)
    mine = lax.all_to_all(payload, "tp", 0, 0, axis_index_groups=X_GROUPS, tiled=True)
    own_weight, other_weight = call(
        columns_kernel, "columns", [SMEM, VMEM], [((W, XS * W), BF16)] * 2, 1, core, out_weight
    )
    other_weight = lax.ppermute(other_weight, "tp", SWAP)
    mine, core, group, own_weight, other_weight = lax.optimization_barrier(
        (mine, core, group, own_weight, other_weight)
    )
    theirs = lax.ppermute(mine, "tp", SWAP)
    half, narrow, steps_weight = call(
        half_kernel,
        "half",
        [SMEM, VMEM, VMEM, VMEM],
        [((L, 2 * W), F32), ((144, L), F32), ((SLICE, D), BF16)],
        1 << 30,
        core, mine, flat_weight, steps_weight,
        scratch=[pltpu.VMEM((SLICE, D), F32)],
    )
    values, gates, query, key, rows, message = call(
        project_kernel,
        "project",
        [SMEM, SMEM, SMEM, VMEM, VMEM, VMEM, VMEM, VMEM, VMEM],
        [
            ((L, W), BF16),
            ((L, W), F32),
            ((L, N), BF16),
            ((N, L), BF16),
            ((32, L), F32),
            ((GROUP, SLICE, 2 * W + N), BF16),
        ],
        1 << 31,
        core, dt_bias, decay_rate, mine, theirs, flat_weight, steps_weight, half, narrow,
    )
    near = lax.all_to_all(message, "seq", 0, 0, axis_index_groups=NEAR, tiled=True)
    (inner,) = call(
        inner_kernel,
        "inside",
        [SMEM, VMEM, VMEM, VMEM, VMEM],
        [((L, W), F32)],
        1 << 31,
        skip_gain, query, key, values, rows,
        scratch=[pltpu.VMEM((L, N), F32)],
    )
    (totals,) = call(
        totals_kernel, "totals", [SMEM, VMEM], [((8, SLICE, W + N), BF16)], 1 << 20, group, near
    )
    far = lax.all_to_all(totals, "seq", 0, 0, axis_index_groups=FAR, tiled=True)
    far, inner = lax.optimization_barrier((far, inner))
    (enters,) = call(
        enter_kernel, "enters", [SMEM, VMEM, VMEM], [((GROUP, SLICE, 2 * W), BF16)], 1 << 20, group, near, far
    )
    enter = lax.all_to_all(enters, "seq", 0, 0, axis_index_groups=NEAR, tiled=True).reshape(N, 2 * W)
    (hidden,) = call(
        mix_kernel, "mix", [VMEM] * 5, [((L, W), BF16)], 1 << 28, inner, gates, query, enter, rows
    )
    hidden = lax.all_gather(hidden, "tp", axis_index_groups=PAIRS)
    (paired,) = call(
        pair_kernel, "pair", [SMEM, VMEM, VMEM, VMEM], [((XS, L, W), BF16)], 1 << 29, core, hidden, own_weight, other_weight,
        touched=1 << 25,
    )
    pieces = lax.all_to_all(paired, "tp", 0, 0, axis_index_groups=SUM_GROUPS, tiled=True)
    return call(sum_kernel, "sum", [VMEM], [((L, W), BF16)], 1 << 20, pieces)[0]


def solution(mesh):
    in_specs = (
        P("seq", "tp"),
        P(None, None, "tp"),
        P(None, "tp"),
        P(None, None, "tp"),
        P(None, "tp"),
        P("tp"),
        P("tp"),
        P("tp", None),
    )
    out_specs = P("seq", "tp")
    return jax.shard_map(shards, mesh=mesh, in_specs=in_specs, out_specs=out_specs, check_vma=False)
```

```python
import jax
import jax.numpy as jnp
from jax import lax
from jax.experimental import pallas as pl
from jax.experimental.pallas import tpu as pltpu
from jax.sharding import PartitionSpec as P

F32 = jnp.float32
BF16 = jnp.bfloat16
L = 512
D = 2048
W = 256
H = 4
HD = 64
N = 128
XS = 4
GROUP = 8
SLICE = N // GROUP
FAR_ROWS = SLICE * (W // N) + 8

X_ORDER = [2, 3, 1, 0]
X_GROUPS = [[2 * x + c for x in X_ORDER] for c in range(2)]
SUM_ORDER = [2, 3, 1, 0]
SUM_GROUPS = [[2 * x + c for x in SUM_ORDER] for c in range(2)]
PAIRS = [[2 * x, 2 * x + 1] for x in range(XS)]
SWAP = [(i, i ^ 1) for i in range(8)]
NEAR_ORDER = [6, 7, 5, 4, 3, 2, 1, 0]
NEAR = [[GROUP * g + j for j in NEAR_ORDER] for g in range(8)]
FAR_ORDER = [5, 6, 4, 7, 3, 0, 2, 1]
FAR = [[GROUP * g + j for g in FAR_ORDER] for j in range(GROUP)]

VMEM = pl.BlockSpec(memory_space=pltpu.VMEM)
SMEM = pl.BlockSpec(memory_space=pltpu.SMEM)
HBM = pl.BlockSpec(memory_space=pltpu.HBM)
NN = (((1,), (0,)), ((), ()))
NT = (((1,), (1,)), ((), ()))


def dot(a, b, dims=NN):
    return lax.dot_general(a, b, dims, preferred_element_type=F32)


def iota(shape, axis):
    return lax.broadcasted_iota(jnp.int32, shape, axis)


def spread(width, base, copies):
    row = iota((N, width), 0)
    want = iota((N, width), 1) // HD + base
    hit = row == want
    for q in range(1, copies):
        hit = hit | (row == want + 8 * q)
    return hit.astype(BF16)


def widen(cols, base, width):
    pick = spread(width, base, 1)
    high = cols.astype(BF16)
    low = (cols - high.astype(F32)).astype(BF16)
    return dot(high, pick) + dot(low, pick)


def column(ref, rows):
    index = iota((2 * H, 1), 0)
    out = jnp.zeros((2 * H, 1), F32)
    for i in range(2 * H):
        out = jnp.where(index == i, rows(ref, i), out)
    return out


def prep_kernel(tokens_ref, bc_ref, out_ref, tokens_here, bc_here, rows_ref, in_sems, sems):
    half = L // 2
    reads = [pltpu.make_async_copy(bc_ref, bc_here, in_sems.at[2])]
    for i in range(2):
        part = pl.ds(half * i, half)
        reads.append(pltpu.make_async_copy(tokens_ref.at[part], tokens_here.at[part], in_sems.at[i]))
    for read in reads:
        read.start()
    copies = []

    def spread_out(source, first):
        for x in range(XS):
            copies.append(pltpu.make_async_copy(source, out_ref.at[x, pl.ds(first, W)], sems.at[len(copies)]))
            copies[-1].start()

    reads[0].wait()
    for b in range(8):
        rows_ref[32 * b : 32 * (b + 1), :] = bc_here[:, W * b : W * (b + 1)]
    spread_out(rows_ref, L)
    for i in range(2):
        reads[1 + i].wait()
        spread_out(tokens_here.at[pl.ds(half * i, half)], half * i)
    for copy in copies:
        copy.wait()


def columns_kernel(core_ref, w_ref, own_ref, out_ref):
    for x in range(XS):
        for ref, c in ((own_ref, core_ref[0]), (out_ref, 1 - core_ref[0])):
            ref[:, W * x : W * (x + 1)] = w_ref[:, pl.ds(pl.multiple_of((2 * x + c) * W, W), W)]


def bc_columns(ref, first, j):
    row = pl.multiple_of(L + j * 32, 32)
    return [ref[X_ORDER.index(x), pl.ds(row, 32), :] for x in (first, first + 1)]


def wide_part(ref, w_ref, c):
    total = None
    for x in range(XS):
        rows = pl.ds(pl.multiple_of((2 * x + c) * W, W), W)
        term = dot(ref[X_ORDER.index(x), 0:L, :], w_ref[rows, :])
        total = term if total is None else total + term
    return total


def narrow_part(ref, refs, d_ref, c):
    total = None
    for x in range(XS):
        j = 2 * x + c
        pieces = [piece for first in (0, 2) for r in refs for piece in bc_columns(r, first, j)]
        if d_ref is not None:
            pieces.append(d_ref[:, pl.ds(pl.multiple_of(j * W, W), W)])
        term = dot(jnp.concatenate(pieces, axis=0), ref[X_ORDER.index(x), 0:L, :], NT)
        total = term if total is None else total + term
    return total


def half_kernel(core_ref, a_ref, w_ref, d_ref, wide_ref, narrow_ref, steps_ref, high_ref):
    c = core_ref[0]
    high_ref[...] = jnp.zeros((SLICE, D), F32)
    for i in range(2):
        high_ref[H * i : H * (i + 1), :] = d_ref[i].astype(F32)
    steps_ref[...] = high_ref[...].astype(BF16)
    wide_ref[...] = wide_part(a_ref, w_ref, c)
    narrow_ref[...] = narrow_part(a_ref, (a_ref,), steps_ref, c)


def project_kernel(
    core_ref, bias_ref, rate_ref, a_ref, b_ref, w_ref, d_ref, half_ref, narrow_ref,
    values_ref, gates_ref, query_ref, key_ref, rows_ref, message_ref,
):
    c = core_ref[0]
    later = narrow_part(b_ref, (a_ref, b_ref), d_ref, 1 - c)
    earlier = narrow_ref[...]
    crossed = narrow_part(a_ref, (b_ref,), None, c)
    key = jnp.concatenate([earlier[0:64] + later[0:64], crossed[0:64] + later[64:128]], axis=0).astype(BF16)
    key_ref[...] = key
    query = jnp.concatenate([earlier[64:128] + later[128:192], crossed[64:128] + later[192:256]], axis=0)
    query_ref[...] = query.T.astype(BF16)
    both = half_ref[...] + wide_part(b_ref, w_ref, 1 - c)
    gates_ref[...] = both[:, W:]
    values = both[:, :W].astype(BF16)
    values_ref[...] = values
    raw = (earlier[128:136] + later[256:264]) + column(bias_ref, lambda r, i: r[i // H, i % H])
    steps = jnp.maximum(raw, 0.0) + jnp.log1p(jnp.exp(-jnp.abs(raw)))
    logs = -column(rate_ref, lambda r, i: r[i % H]) * steps
    p1 = logs.astype(BF16)
    rest = logs - p1.astype(F32)
    p2 = rest.astype(BF16)
    p3 = (rest - p2.astype(F32)).astype(BF16)
    running = (iota((L, L), 0) <= iota((L, L), 1)).astype(BF16)
    parts = jnp.concatenate([p1.astype(F32), p2.astype(F32), p3.astype(F32), jnp.zeros((8, L), F32)], axis=0)
    summed = dot(parts.astype(BF16), running)
    upto = summed[0:8] + summed[8:16] + summed[16:24]
    before = upto - logs
    total = upto[:, L - 1 : L]
    forward = iota((2 * H, L), 0) < H
    scale = jnp.exp(jnp.where(forward, total - upto, before)) * steps
    reach = jnp.exp(jnp.where(forward, before, total - upto))
    rows_ref[...] = jnp.concatenate([upto, before, steps, reach], axis=0)

    wide = key.astype(F32)
    scaled = jnp.concatenate([(wide * scale[i : i + 1]).astype(BF16) for i in range(2 * H)], axis=0)
    state = dot(scaled, values)
    head = iota((N, W), 1) // HD
    sides = []
    for first in (0, H):
        out = state[N * first : N * (first + 1)]
        for h in range(1, H):
            out = jnp.where(head == h, state[N * (first + h) : N * (first + h + 1)], out)
        sides.append(out.astype(BF16))
    lane = iota((2 * H, N), 1)
    mine_only = (iota((2 * H, N), 0) == lane % 8) & (lane < 16)
    last = jnp.sum(jnp.where(mine_only, total, 0.0), axis=0, keepdims=True)
    high = last.astype(BF16).astype(F32)
    extra = jnp.where(iota((1, N), 1) < 8, high, last - high)
    extra = jnp.broadcast_to(extra, (SLICE, N)).astype(BF16)
    for k in range(GROUP):
        for i in range(2):
            message_ref[k, :, W * i : W * (i + 1)] = sides[i][SLICE * k : SLICE * (k + 1)]
        message_ref[k, :, 2 * W : 2 * W + N] = extra


def inner_kernel(skip_ref, query_ref, key_ref, values_ref, rows_ref, inner_ref, cols_ref):
    cols_ref[...] = jnp.concatenate([rows_ref[...], jnp.zeros((N - 32, L), F32)], axis=0).T
    tile = 128
    lane = iota((tile, W), 1) // HD
    gain = jnp.zeros((1, W), F32)
    for h in range(H):
        gain = jnp.where(iota((1, W), 1) // HD == h, skip_ref[h], gain)
    lower = iota((tile, tile), 0) > iota((tile, tile), 1)
    upper = iota((tile, tile), 0) < iota((tile, tile), 1)
    for i in range(L // tile):
        first, last = i * tile, (i + 1) * tile
        here = slice(first, last)
        scores = dot(query_ref[here, :], key_ref[...])
        cols = cols_ref[here, :]
        since = jnp.exp(cols - cols[0:1])
        until = jnp.exp(cols[tile - 1 : tile] - cols)
        if i > 0:
            edge = rows_ref[0:H, first - 1 : first]
            past = jnp.exp(edge - rows_ref[0:H, 0:first]) * rows_ref[16 : 16 + H, 0:first]
        if last < L:
            edge = rows_ref[H : 2 * H, last - 1 : last]
            coming = jnp.exp(rows_ref[12 : 12 + H, last:L] - edge) * rows_ref[20 : 20 + H, last:L]
        out = jnp.zeros((tile, W), F32)
        for h in range(H):
            gap = jnp.where(
                lower,
                cols[:, 8 + h : 9 + h] - rows_ref[h : h + 1, here],
                rows_ref[12 + h : 13 + h, here] - cols[:, H + h : H + h + 1],
            )
            step = jnp.where(lower, rows_ref[16 + h : 17 + h, here], rows_ref[20 + h : 21 + h, here])
            own = jnp.where(lower | upper, scores[:, here] * jnp.exp(gap) * step, 0.0).astype(BF16)
            pieces = [own]
            if i > 0:
                pieces.insert(0, (scores[:, 0:first] * past[h : h + 1] * since[:, 8 + h : 9 + h]).astype(BF16))
            if last < L:
                pieces.append((scores[:, last:L] * coming[h : h + 1] * until[:, H + h : H + h + 1]).astype(BF16))
            out = jnp.where(lane == h, dot(jnp.concatenate(pieces, axis=1), values_ref[...]), out)
        inner_ref[here, :] = out + gain * values_ref[here, :].astype(F32)


def near_states(got_ref):
    extra = got_ref[:, :, 2 * W : 2 * W + N].reshape(GROUP * SLICE, N)
    decay = jnp.exp(dot(extra, spread(2 * W, 0, 2)))
    order = [NEAR_ORDER.index(j) for j in range(GROUP)]
    states = [got_ref[j, :, 0 : 2 * W].astype(F32) for j in order]
    decays = [decay[SLICE * j : SLICE * (j + 1)] for j in order]
    return states, decays


def totals_kernel(group_ref, got_ref, out_ref):
    g = group_ref[0]
    states, decays = near_states(got_ref)
    forward = states[0][:, :W]
    for j in range(1, GROUP):
        forward = decays[j][:, :W] * forward + states[j][:, :W]
    backward = states[GROUP - 1][:, W:]
    for j in range(GROUP - 2, -1, -1):
        backward = decays[j][:, W:] * backward + states[j][:, W:]
    log = jnp.zeros((SLICE, N), F32)
    for j in range(GROUP):
        log = log + got_ref[j, :, 2 * W : 2 * W + N].astype(F32)
    high = log.astype(BF16).astype(F32)
    log = (high + pltpu.roll(log - high, 16, 1)).astype(BF16)
    forward = forward.astype(BF16)
    backward = backward.astype(BF16)
    for q in range(8):
        chosen = jnp.where(FAR_ORDER[q] > g, forward, backward)
        for i in range(W // N):
            out_ref[q, SLICE * i : SLICE * (i + 1), :] = chosen[:, N * i : N * (i + 1)]
        out_ref[q, FAR_ROWS - 8 : FAR_ROWS, :] = log[0:8]


def enter_kernel(group_ref, got_ref, far_ref, out_ref):
    g = group_ref[0]
    states, decays = near_states(got_ref)
    extra = far_ref[:, FAR_ROWS - 8 : FAR_ROWS, :].astype(F32).reshape(64, N).astype(BF16)
    decay = jnp.exp(dot(extra, spread(2 * W, 0, 4)))

    def total(slot):
        parts = [far_ref[slot, SLICE * i : SLICE * (i + 1), :] for i in range(W // N)]
        return jnp.concatenate(parts, axis=1).astype(F32)

    forward = jnp.zeros((SLICE, W), F32)
    backward = jnp.zeros((SLICE, W), F32)
    for q in range(8):
        slot = FAR_ORDER.index(q)
        rows = slice(8 * slot, 8 * slot + 1)
        forward = jnp.where(q < g, decay[rows, :W] * forward + total(slot), forward)
    for q in range(7, -1, -1):
        slot = FAR_ORDER.index(q)
        rows = slice(8 * slot, 8 * slot + 1)
        backward = jnp.where(q > g, decay[rows, W:] * backward + total(slot), backward)
    for j in range(GROUP):
        out_ref[NEAR_ORDER.index(j), :, 0:W] = forward.astype(BF16)
        forward = decays[j][:, :W] * forward + states[j][:, :W]
    for j in range(GROUP - 1, -1, -1):
        out_ref[NEAR_ORDER.index(j), :, W : 2 * W] = backward.astype(BF16)
        backward = decays[j][:, W:] * backward + states[j][:, W:]


def mix_kernel(inner_ref, gates_ref, query_ref, enter_ref, rows_ref, hidden_ref):
    cols = jnp.concatenate([rows_ref[24:32], jnp.zeros((N - 8, L), F32)], axis=0).T
    carried = dot(query_ref[...], enter_ref[...]) * widen(cols, 0, 2 * W)
    mix = inner_ref[...] + carried[:, :W] + carried[:, W:]
    gates = gates_ref[...]
    gated = mix * (gates / (1.0 + jnp.exp(-gates)))
    square = gated * gated
    same = (iota((W, W), 0) // HD == iota((W, W), 1) // HD).astype(BF16)
    high = square.astype(BF16)
    low = (square - high.astype(F32)).astype(BF16)
    power = (dot(high, same) + dot(low, same)) * (1.0 / HD)
    hidden_ref[...] = (gated * lax.rsqrt(power + 1e-05)).astype(BF16)


def pair_kernel(core_ref, hidden_ref, w_ref, other_ref, out_ref):
    c = core_ref[0]
    hidden = jnp.concatenate([hidden_ref[c], hidden_ref[1 - c]], axis=1)
    for x in range(XS):
        at = slice(W * x, W * (x + 1))
        out_ref[SUM_ORDER.index(x)] = dot(hidden, jnp.concatenate([w_ref[:, at], other_ref[:, at]], axis=0)).astype(BF16)


def sum_kernel(pieces_ref, out_ref, staged_ref, sems):
    rows = L // 4
    copies = []
    for i in range(4):
        at = slice(rows * i, rows * (i + 1))
        total = pieces_ref[0, at].astype(F32) + pieces_ref[1, at].astype(F32)
        total = total + pieces_ref[2, at].astype(F32) + pieces_ref[3, at].astype(F32)
        staged_ref[at] = total.astype(BF16)
        part = pl.ds(rows * i, rows)
        copies.append(pltpu.make_async_copy(staged_ref.at[part], out_ref.at[part], sems.at[i]))
        copies[-1].start()
    for copy in copies:
        copy.wait()


def call(kernel, name, ins, outs, flops, *operands, touched=1 << 21, scratch=(), out_spec=VMEM, limit=20 << 20):
    return pl.pallas_call(
        kernel,
        name=name,
        in_specs=ins,
        out_specs=[out_spec] * len(outs),
        scratch_shapes=scratch,
        out_shape=[jax.ShapeDtypeStruct(shape, kind) for shape, kind in outs],
        compiler_params=pltpu.CompilerParams(vmem_limit_bytes=limit),
        cost_estimate=pl.CostEstimate(flops=flops, bytes_accessed=touched, transcendentals=1 << 16),
    )(*operands)


def shards(tokens, in_weight, bc_weight, dt_weight, dt_bias, decay_rate, skip_gain, out_weight):
    core = (lax.axis_index("tp").astype(jnp.int32) & 1)[None]
    group = (lax.axis_index("seq").astype(jnp.int32) >> 3)[None]
    (payload,) = call(
        prep_kernel,
        "payload",
        [HBM, HBM],
        [((XS, L + W, W), BF16)],
        1,
        tokens,
        bc_weight.T,
        touched=0,
        scratch=[
            pltpu.VMEM((L, W), BF16),
            pltpu.VMEM((32, D), BF16),
            pltpu.VMEM((W, W), BF16),
            pltpu.SemaphoreType.DMA((3,)),
            pltpu.SemaphoreType.DMA((3 * XS,)),
        ],
        out_spec=HBM,
        limit=(64 << 20) - (64 << 10),
    )
    flat_weight = in_weight.reshape(D, 2 * W)
    steps_weight = dt_weight.transpose(0, 2, 1)
    mine = lax.all_to_all(payload, "tp", 0, 0, axis_index_groups=X_GROUPS, tiled=True)
    own_weight, other_weight = call(
        columns_kernel, "columns", [SMEM, VMEM], [((W, XS * W), BF16)] * 2, 1, core, out_weight
    )
    other_weight = lax.ppermute(other_weight, "tp", SWAP)
    mine, core, group, own_weight, other_weight = lax.optimization_barrier(
        (mine, core, group, own_weight, other_weight)
    )
    theirs = lax.ppermute(mine, "tp", SWAP)
    half, narrow, steps_weight = call(
        half_kernel,
        "half",
        [SMEM, VMEM, VMEM, VMEM],
        [((L, 2 * W), F32), ((144, L), F32), ((SLICE, D), BF16)],
        1 << 30,
        core, mine, flat_weight, steps_weight,
        scratch=[pltpu.VMEM((SLICE, D), F32)],
    )
    values, gates, query, key, rows, message = call(
        project_kernel,
        "project",
        [SMEM, SMEM, SMEM, VMEM, VMEM, VMEM, VMEM, VMEM, VMEM],
        [
            ((L, W), BF16),
            ((L, W), F32),
            ((L, N), BF16),
            ((N, L), BF16),
            ((32, L), F32),
            ((GROUP, SLICE, 2 * W + N), BF16),
        ],
        1 << 31,
        core, dt_bias, decay_rate, mine, theirs, flat_weight, steps_weight, half, narrow,
    )
    near = lax.all_to_all(message, "seq", 0, 0, axis_index_groups=NEAR, tiled=True)
    (inner,) = call(
        inner_kernel,
        "inside",
        [SMEM, VMEM, VMEM, VMEM, VMEM],
        [((L, W), F32)],
        1 << 31,
        skip_gain, query, key, values, rows,
        scratch=[pltpu.VMEM((L, N), F32)],
    )
    (totals,) = call(
        totals_kernel, "totals", [SMEM, VMEM], [((8, FAR_ROWS, N), BF16)], 1 << 20, group, near
    )
    far = lax.all_to_all(totals, "seq", 0, 0, axis_index_groups=FAR, tiled=True)
    far, inner = lax.optimization_barrier((far, inner))
    (enters,) = call(
        enter_kernel, "enters", [SMEM, VMEM, VMEM], [((GROUP, SLICE, 2 * W), BF16)], 1 << 20, group, near, far
    )
    enter = lax.all_to_all(enters, "seq", 0, 0, axis_index_groups=NEAR, tiled=True).reshape(N, 2 * W)
    (hidden,) = call(
        mix_kernel, "mix", [VMEM] * 5, [((L, W), BF16)], 1 << 28, inner, gates, query, enter, rows
    )
    hidden = lax.all_gather(hidden, "tp", axis_index_groups=PAIRS)
    (paired,) = call(
        pair_kernel, "pair", [SMEM, VMEM, VMEM, VMEM], [((XS, L, W), BF16)], 1 << 29, core, hidden, own_weight, other_weight,
        touched=1 << 25,
    )
    pieces = lax.all_to_all(paired, "tp", 0, 0, axis_index_groups=SUM_GROUPS, tiled=True)
    return call(
        sum_kernel,
        "sum",
        [VMEM],
        [((L, W), BF16)],
        1 << 20,
        pieces,
        scratch=[pltpu.VMEM((L, W), BF16), pltpu.SemaphoreType.DMA((4,))],
        out_spec=HBM,
    )[0]


def solution(mesh):
    in_specs = (
        P("seq", "tp"),
        P(None, None, "tp"),
        P(None, "tp"),
        P(None, None, "tp"),
        P(None, "tp"),
        P("tp"),
        P("tp"),
        P("tp", None),
    )
    out_specs = P("seq", "tp")
    return jax.shard_map(shards, mesh=mesh, in_specs=in_specs, out_specs=out_specs, check_vma=False)
```
